768 devices in a mesh: layer: 4 (over y_lo), gx: 24 (over z, core), gy: 8 (over x, y_hi).
Axes of the slice: x: 4, y: 8 (y_hi: 2, y_lo: 4; y = y_hi * 4 + y_lo), z: 12, core: 2. Of those that a mesh axis runs over, the one named last changes fastest.
Arguments:
- wave: bfloat16 [13, 4, 24, 6, 6, 6, 1024], P(None, 'layer', 'gx', None, None, None, 'gy'), may hold values from -36 to 36
- adjoint_source: bfloat16 [13, 4, 24, 6, 6, 6, 1024], P(None, 'layer', 'gx', None, None, None, 'gy'), may hold values from -36 to 36
- coupling: float32 [4, 3, 13, 13], P('layer'), may hold values from -1 to 1
- stiffness: float32 [13, 4, 24, 1024], P(None, 'layer', 'gx', 'gy'), may hold values from 0.5 to 2
- partner: int32 [4, 24, 1024], P(None, 'gx', 'gy'), may hold values from 0 to 3, as said below
- owner: int32 [4, 24, 1024], P('layer', 'gx', 'gy'), may hold values from 0 to 1023
Outputs:
- final_wave: bfloat16 [13, 4, 24, 6, 6, 6, 1024], P(None, 'layer', 'gx', None, None, None, 'gy')
- adjoint_wave: bfloat16 [13, 4, 24, 6, 6, 6, 1024], P(None, 'layer', 'gx', None, None, None, 'gy')
- cell_kernel: float32 [4, 24, 13, 1024], P('layer', 'gx', None, 'gy')
The draws below stay inside these ranges and needn't reach their ends.
Inputs may be any that keep to these rules, and one draw needn't show every extreme that they name: `partner`: in every element column each depth group is named exactly once.
All inputs are finite; a program needn't handle non-finite values.
Results may differ from the reference program's by a relative error of at most 0.005.
Values may be sent and summed in bfloat16 or wider, within the bound.
No kernel may reach another device: no remote copies, remote signals or barrier semaphores. Data moves between devices by JAX's collectives and lax.ppermute only.
A program may use at most 128 MiB of HBM per device.

```python
import math
import jax
import jax.numpy as jnp
import numpy as np
from jax import lax

F = 13
NP = 6
STEPS = 1
EX = 1
EY = 128
GROUPS = 4
STRIPS = 24
NXE = 24
NYE = 1024
CELLS = 1024


def border_factor():
    column = jnp.arange(NYE, dtype=jnp.int32) % EY
    return jnp.where((column == 0) | (column == EY - 1), 6.0, 1.0).astype(jnp.float32)


def draw_wave(key, part):
    key = jax.random.fold_in(key, 11)
    shape = (F, GROUPS, NXE, NP, NP, NP, NYE)
    values = jnp.clip(jax.random.normal(key, shape, jnp.float32), -6.0, 6.0)
    return (values * border_factor()).astype(jnp.bfloat16)


def draw_adjoint_source(key, part):
    key = jax.random.fold_in(key, 23)
    shape = (F, GROUPS, NXE, NP, NP, NP, NYE)
    values = jnp.clip(jax.random.normal(key, shape, jnp.float32), -6.0, 6.0)
    return (values * border_factor()).astype(jnp.bfloat16)


def draw_partner(key, part):
    key = jax.random.fold_in(key, 37)
    scores = jax.random.randint(key, (GROUPS, NXE, NYE), 0, 1048576, jnp.int32)
    scores = scores * GROUPS + jnp.arange(GROUPS, dtype=jnp.int32)[:, None, None]
    return jnp.argsort(scores, axis=0, stable=True).astype(jnp.int32)


def place_ends(values, key, smallest, largest):
    longest = values.shape.index(max(values.shape))
    spots = []
    for shift in (0, 1):
        where = [jax.random.randint(jax.random.fold_in(key, axis), (), 0, length) for axis, length in enumerate(values.shape)]
        where[longest] = (where[longest] + shift) % values.shape[longest]
        spots.append(tuple(where))
    return values.at[spots[0]].set(smallest).at[spots[1]].set(largest)


def level_of(own_key, dims, shards, low, largest):
    loudness, own = 1.0, jax.random.fold_in(own_key, 6)
    for dim, blocks in shards:
        draws = jnp.exp(jax.random.uniform(jax.random.fold_in(own, dim), (blocks,), jnp.float32, low / len(shards), largest / len(shards)))
        loudness = loudness * jnp.repeat(draws, dims[dim] // blocks).reshape([-1 if axis == dim else 1 for axis in range(len(dims))])
    return loudness


def rank_bounds(count, skew):
    loads = [(1 << 20) // math.isqrt(rank ** skew) + 1 for rank in range(1, count + 1)]
    scale = 1 + sum(loads) // (1 << 30)
    return np.cumsum(np.array([max(1, weight // scale) for weight in loads]))


def ranked_ids(stream_key, shape, amount, slope):
    grid = rank_bounds(amount, slope)
    ticket = jax.random.randint(jax.random.fold_in(stream_key, 1), shape, 0, int(grid[amount - 1]))
    standing = jnp.searchsorted(jnp.asarray(grid, jnp.int32), ticket, side="right")
    return jax.random.permutation(jax.random.fold_in(stream_key, 2), amount)[standing].astype(jnp.int32)


def normal_values(key, dims, spread, reach, cuts=(), held_as=jnp.bfloat16):
    values = spread * jax.random.normal(key, dims, jnp.float32)
    if cuts:
        values = values * level_of(key, dims, cuts, -0.22, 0.18)
    return jnp.clip(values, -reach, reach).astype(held_as)


def setup_inputs(seed: int = 0) -> dict:
    key_list = jax.random.split(jax.random.key(seed), 7)
    wave = draw_wave(jax.random.fold_in(key_list[6], 71), 0)
    adjoint_source = draw_adjoint_source(jax.random.fold_in(key_list[6], 71), 0)
    coupling = normal_values(key_list[2], (GROUPS, 3, F, F), (3 * F) ** -0.5, 1.0, ((0, 4),), jnp.float32)
    stiffness = jnp.clip(jnp.exp(math.log(2.0) - 1.3862944 * jax.random.uniform(key_list[3], (F, GROUPS, NXE, NYE), jnp.float32) ** level_of(key_list[3], (F, GROUPS, NXE, NYE), ((1, 4), (2, 24), (3, 8)), -0.2, 0.2)), 0.5, 2.0)
    partner = draw_partner(jax.random.fold_in(key_list[6], 71), 0)
    owner = place_ends(ranked_ids(key_list[5], (GROUPS, NXE, NYE), CELLS, 2), jax.random.fold_in(key_list[5], 3), 0, CELLS - 1).astype(jnp.int32)
    return dict(wave=wave, adjoint_source=adjoint_source, coupling=coupling, stiffness=stiffness, partner=partner, owner=owner)


HIGH = lax.Precision.HIGHEST
DT = 0.05
TAU = 7.5

def lobatto_derivative():
    outer = math.sqrt(1.0 / 3.0 + 2.0 * math.sqrt(7.0) / 21.0)
    inner = math.sqrt(1.0 / 3.0 - 2.0 * math.sqrt(7.0) / 21.0)
    nodes = np.array([-1.0, -outer, -inner, inner, outer, 1.0])
    weights = np.array([1.0 / np.prod([nodes[col] - nodes[other] for other in range(6) if other != col]) for col in range(6)])
    table = np.zeros((6, 6))
    for row_id in range(6):
        for col in range(6):
            if row_id != col:
                table[row_id, col] = weights[col] / weights[row_id] / (nodes[row_id] - nodes[col])
        table[row_id, row_id] = -np.sum(table[row_id])
    return table

def interior(field, matrices, adjoint):
    table = jnp.asarray(lobatto_derivative(), jnp.float32)
    slopes = (jnp.einsum('ia,fxabcy->fxibcy', table, field, precision=HIGH), jnp.einsum('ib,fxabcy->fxaicy', table, field, precision=HIGH), jnp.einsum('ic,fxabcy->fxabiy', table, field, precision=HIGH))
    total = jnp.zeros_like(field)
    for direction in range(3):
        if adjoint:
            total = total - jnp.einsum('hf,hxabcy->fxabcy', matrices[direction], slopes[direction], precision=HIGH)
        else:
            total = total + jnp.einsum('fh,hxabcy->fxabcy', matrices[direction], slopes[direction], precision=HIGH)
    return total

def face_terms(field, x_low, x_high, y_low, y_high, floor_trace):
    zero_a = jnp.zeros_like(field[:, :, 1:5])
    term_a = jnp.concatenate([(x_low - field[:, :, 0])[:, :, None], zero_a, (x_high - field[:, :, 5])[:, :, None]], axis=2)
    zero_b = jnp.zeros_like(field[:, :, :, 1:5])
    term_b = jnp.concatenate([(y_low - field[:, :, :, 0])[:, :, :, None], zero_b, (y_high - field[:, :, :, 5])[:, :, :, None]], axis=3)
    top = jnp.concatenate([floor_trace - field[0:4, :, :, :, 5], jnp.zeros_like(field[4:, :, :, :, 5])], axis=0)
    term_c = jnp.concatenate([jnp.zeros_like(field[:, :, :, :, 0:5]), top[:, :, :, :, None]], axis=4)
    return TAU * (term_a + term_b + term_c)

def lateral(field):
    high_x = field[:, :, 5]
    low_x = field[:, :, 0]
    x_low = jnp.concatenate([jnp.zeros_like(high_x[:, 0:1]), high_x[:, :-1]], axis=1)
    x_high = jnp.concatenate([low_x[:, 1:], jnp.zeros_like(low_x[:, 0:1])], axis=1)
    high_y = field[:, :, :, 5]
    low_y = field[:, :, :, 0]
    y_low = jnp.concatenate([jnp.zeros_like(high_y[..., 0:1]), high_y[..., :-1]], axis=4)
    y_high = jnp.concatenate([low_y[..., 1:], jnp.zeros_like(low_y[..., 0:1])], axis=4)
    return (x_low, x_high, y_low, y_high)

def floors_of(fields, partner):
    bottoms = jnp.stack([lax.optimization_barrier(field[0:4, :, :, :, 0].astype(jnp.bfloat16)).astype(jnp.float32) for field in fields])
    count = len(fields)
    group_ids = jnp.arange(count, dtype=jnp.int32).reshape(count, 1, 1, 1, 1, 1)
    result = []
    for index in range(count):
        pick = partner[index][None, None, :, None, None, :] == group_ids
        result.append(lax.optimization_barrier(jnp.sum(jnp.where(pick, bottoms, jnp.float32(0.0)), axis=0)))
    return result

def rates_of(fields, coupling, partner, adjoint):
    floors = floors_of(fields, partner)
    result = []
    for index in range(len(fields)):
        x_low, x_high, y_low, y_high = lateral(fields[index])
        inner_rate = interior(fields[index], coupling[index], adjoint)
        result.append(inner_rate + face_terms(fields[index], x_low, x_high, y_low, y_high, floors[index]))
    return result

def reference(wave, adjoint_source, coupling, stiffness, partner, owner):
    groups = wave.shape[1]
    states = [wave[:, index].astype(jnp.float32) for index in range(groups)]
    scales = [stiffness[:, index][:, :, None, None, None, :] for index in range(groups)]
    history = []
    for step in range(STEPS):
        rates = rates_of(states, coupling, partner, False)
        history.append(rates)
        states = [states[index] + DT * scales[index] * rates[index] for index in range(groups)]
    final_wave = jnp.stack(states, axis=1).astype(jnp.bfloat16)
    adjoints = [adjoint_source[:, index].astype(jnp.float32) for index in range(groups)]
    kernels = [jnp.zeros_like(stiffness[:, index]) for index in range(groups)]
    for step in reversed(range(STEPS)):
        kernels = [kernels[index] + DT * lax.optimization_barrier(jnp.sum(adjoints[index] * history[step][index], axis=(2, 3, 4))) for index in range(groups)]
        scaled = [scales[index] * adjoints[index] for index in range(groups)]
        back = rates_of(scaled, coupling, partner, True)
        adjoints = [adjoints[index] + DT * back[index] for index in range(groups)]
    adjoint_wave = jnp.stack(adjoints, axis=1).astype(jnp.bfloat16)
    element_kernel = jnp.stack(kernels, axis=1)
    flat_kernel = element_kernel.reshape(F, GROUPS, STRIPS, EX, NYE).transpose(1, 2, 3, 4, 0).reshape(-1, F)
    strip_ids = jnp.arange(GROUPS * STRIPS, dtype=jnp.int32).reshape(GROUPS, STRIPS, 1, 1)
    segment = (strip_ids * CELLS + owner.reshape(GROUPS, STRIPS, EX, NYE)).reshape(-1).astype(jnp.int32)
    binned = jax.ops.segment_sum(flat_kernel, segment, num_segments=GROUPS * STRIPS * CELLS)
    cell_kernel = binned.reshape(GROUPS, STRIPS, CELLS, F).transpose(0, 1, 3, 2)
    return (final_wave, adjoint_wave, cell_kernel)
```

```python
import functools
import math

import jax
import jax.numpy as jnp
import numpy as np
from jax import lax
from jax.experimental import pallas as pl
from jax.experimental.pallas import tpu as pltpu
from jax.sharding import PartitionSpec as P

F = 13
ROWS = 16
NP = 6
EY = 128
CELLS_DEV = 128
BOTTOM = 4
HALF = 64
S_RIGHT = 36
S_LEFT = 100
DT = 0.05
TAU = 7.5
F32 = jnp.float32
BF16 = jnp.bfloat16
VMEM_LIMIT = 40 * 1024 * 1024


def lobatto_derivative():
    outer = math.sqrt(1.0 / 3.0 + 2.0 * math.sqrt(7.0) / 21.0)
    inner = math.sqrt(1.0 / 3.0 - 2.0 * math.sqrt(7.0) / 21.0)
    nodes = np.array([-1.0, -outer, -inner, inner, outer, 1.0])
    weights = np.array(
        [
            1.0 / np.prod([nodes[col] - nodes[other] for other in range(6) if other != col])
            for col in range(6)
        ]
    )
    table = np.zeros((6, 6))
    for row_id in range(6):
        for col in range(6):
            if row_id != col:
                table[row_id, col] = weights[col] / weights[row_id] / (nodes[row_id] - nodes[col])
        table[row_id, row_id] = -np.sum(table[row_id])
    return table


def lane_ids(rows):
    return lax.broadcasted_iota(jnp.int32, (rows, EY), 1)


def load_scale(stiff_ref, scale):
    for f in range(F):
        scale[f : f + 1, :] = stiff_ref[f]
    return scale[0:F, :]


def prep_kernel(
    wave_ref, adj_ref, stiff_ref, second_ref, first_ref, bottom_ref,
    raw, kept, low, stiff, scale, rows, trace, sems,
):
    odd = lax.rem(lax.axis_index("gx"), 2)
    near = 5 * (1 - odd)
    far = 5 * odd
    copies = []

    def send(src, dst):
        copies.append(pltpu.make_async_copy(src, dst, sems.at[len(copies)]))
        copies[-1].start()
        return copies[-1]

    arrivals = [
        send(stiff_ref, stiff),
        send(adj_ref.at[:, :, 0], low.at[1]),
        send(wave_ref.at[:, :, 0], low.at[0]),
        send(adj_ref.at[far], raw.at[1]),
        send(adj_ref.at[near], raw.at[0]),
    ]
    arrivals += [send(wave_ref.at[far], kept.at[1]), send(wave_ref.at[near], kept.at[0])]
    leaving = []
    for copy in arrivals[0:3]:
        copy.wait()
    s = load_scale(stiff, scale)
    s4 = s[0:BOTTOM]
    for part in range(2):
        for a in range(NP):
            for b in range(NP):
                x = low[part, a, b].astype(F32)[0:BOTTOM]
                if part == 1:
                    x = x * s4
                k = BOTTOM * (a * NP + b)
                rows[k : k + BOTTOM, :] = x
        trace[part] = rows[...].astype(BF16)
    for group in range(bottom_ref.shape[0]):
        leaving.append(send(trace, bottom_ref.at[group]))
    for out_ref, at in ((second_ref, 1), (first_ref, 0)):
        arrivals[6 - at].wait()
        leaving.append(send(kept.at[at], out_ref.at[0]))
    for out_ref, at in ((second_ref, 1), (first_ref, 0)):
        arrivals[4 - at].wait()
        for b in range(NP):
            for c in range(NP):
                raw[at, b, c] = (raw[at, b, c].astype(F32) * s).astype(BF16)
        leaving.append(send(raw.at[at], out_ref.at[1]))
    for copy in leaving:
        copy.wait()


def build_matrices(side, coup_ref, cs, mats):
    table = lobatto_derivative()
    cs[...] = jnp.zeros_like(cs)
    for d in range(3):
        for f in range(F):
            cs[d, f : f + 1, 0:F] = coup_ref[d, f]
    block = lane_ids(ROWS) // ROWS
    spread = []
    for i in range(NP):
        row = jnp.zeros((ROWS, EY), F32)
        for k in range(NP):
            row = jnp.where(block == k, F32(table[i, k]), row)
        spread.append(row)
    for d in range(3):
        base = cs[d]
        if side == 1:
            base = -jnp.concatenate([base, jnp.zeros((EY - ROWS, EY), F32)], axis=0).T[0:ROWS]
        wide = base
        for k in range(1, NP):
            wide = wide + pltpu.roll(base, ROWS * k, 1)
        for i in range(NP):
            mats[d, ROWS * i : ROWS * (i + 1), :] = (wide * spread[i]).astype(BF16)


def put(edge, tile, frm, to):
    return jnp.where(lane_ids(F) == to, pltpu.roll(tile, (to - frm) % EY, 1), edge)


def inner_kernel(
    wave_ref, adj_ref, stiff_ref, coup_ref,
    new_wave_ref, new_adj_ref, side_out_ref, top_out_ref, strip_out_ref, small_out_ref,
    scale, cs, mats, padded, packed, acc, mid, side_ref, top_ref, strip_ref, small, coup, sems,
):
    copies = []

    def send(src, dst):
        copies.append(pltpu.make_async_copy(src, dst, sems.at[len(copies)]))
        copies[-1].start()
        return copies[-1]

    arrival = send(coup_ref, coup)
    s = load_scale(stiff_ref, scale)
    for a in range(NP):
        padded[:, a, :, :, 8:ROWS, :] = jnp.zeros((2, NP, NP, ROWS - 8, EY), F32)
        for b in range(NP):
            for c in range(NP):
                padded[0, a, b, c, 0:F, :] = wave_ref[a, b, c].astype(F32)
                padded[1, a, b, c, 0:F, :] = adj_ref[a, b, c].astype(F32) * s
        for side in range(2):
            packed[side, a] = padded[side, a].astype(BF16)
    arrival.wait()
    small[0, 0:F, :] = s

    def leave(side, a):
        out_ref = new_adj_ref if side else new_wave_ref
        if a in (0, 5):
            send(side_ref.at[side, a // 5], side_out_ref.at[side, a // 5])
        else:
            send(mid.at[side, a - 1], out_ref.at[a, 1:5, 0:5])
            send(top_ref.at[side, a - 1], top_out_ref.at[side, a - 1])
            send(strip_ref.at[side, a - 1], strip_out_ref.at[side, a - 1])

    for side in range(2):
        inner_side(
            side, adj_ref, s, coup, side_ref, top_ref, strip_ref, small,
            cs, mats, padded.at[side], packed.at[side], acc, mid, leave,
        )
    send(small, small_out_ref)
    for copy in copies[1:]:
        copy.wait()


def inner_side(
    side, adj_ref, s, coup_ref, side_ref, top_ref, strip_ref, small,
    cs, mats, padded, packed, acc, mid, leave,
):
    width = NP * ROWS
    lanes = lane_ids(F)
    row_ids = lax.broadcasted_iota(jnp.int32, (F, EY), 0)

    build_matrices(side, coup_ref, cs, mats)
    m = [mats[d][:, 0:width] for d in range(3)]
    for b in range(NP):
        right = jnp.concatenate([packed[:, b, c].reshape(width, EY) for c in range(NP)], axis=1)
        out = jnp.dot(m[0], right, preferred_element_type=F32)
        for c in range(NP):
            acc[:, b, c] = out[:, c * EY : (c + 1) * EY].reshape(NP, ROWS, EY)

    total = jnp.zeros((F, EY), F32)
    u_edge = jnp.zeros((F, EY), F32)
    lam_edge = jnp.zeros((F, EY), F32)
    edge = jnp.zeros((F, EY), F32)
    for a in range(NP):
        right = jnp.concatenate([packed[a, :, c].reshape(width, EY) for c in range(NP)], axis=1)
        along_b = jnp.dot(m[1], right, preferred_element_type=F32)
        right = jnp.concatenate([packed[a, b].reshape(width, EY) for b in range(NP)], axis=1)
        along_c = jnp.dot(m[2], right, preferred_element_type=F32)
        for b in range(NP):
            for c in range(NP):
                rate = (
                    acc[a, b, c]
                    + along_b[ROWS * b : ROWS * (b + 1), c * EY : (c + 1) * EY]
                    + along_c[ROWS * c : ROWS * (c + 1), b * EY : (b + 1) * EY]
                )[0:F]
                v = padded[a, b, c, 0:F, :]
                face = None
                own = (a in (0, 5)) + (b in (0, 5))
                if b == 0:
                    other = padded[a, 5, c, 0:F, :]
                    face = jnp.where(lanes == 0, 0.0, pltpu.roll(other, 1, 1))
                if b == 5:
                    other = padded[a, 0, c, 0:F, :]
                    face = jnp.where(lanes == EY - 1, 0.0, pltpu.roll(other, EY - 1, 1))
                if own:
                    rate = rate - (TAU * own) * v
                if face is not None:
                    rate = rate + TAU * face
                if c == 5:
                    rate = rate - jnp.where(row_ids < BOTTOM, TAU * v, 0.0)
                k = a * NP + c
                lam = adj_ref[a, b, c].astype(F32)
                if side == 0:
                    total = total + lam * rate
                    new = v + (DT * s) * rate
                else:
                    new = lam + DT * rate
                if a in (0, 5):
                    side_ref[side, a // 5, b, c] = rate.astype(BF16)
                elif c == 5:
                    top_ref[side, a - 1, b] = rate.astype(BF16)
                elif b in (0, 5):
                    strip_ref[side, a - 1, b // 5, c] = new.astype(BF16)
                else:
                    mid[side, a - 1, b - 1, c] = new.astype(BF16)
                if b == 0 and a not in (0, 5) and c != 5:
                    edge = put(edge, new, 0, HALF * (1 - side) + k)
                if b == 5 and a not in (0, 5) and c != 5:
                    edge = put(edge, new, EY - 1, HALF * side + k)
                if side == 0 and b == 0:
                    u_edge = put(u_edge, v, 0, k)
                    lam_edge = put(lam_edge, lam, 0, HALF + k)
                if side == 0 and b == 5:
                    u_edge = put(u_edge, v, EY - 1, HALF + k)
                    lam_edge = put(lam_edge, lam, EY - 1, k)
        leave(side, a)
    small[1 + side, 0:F, :] = edge
    if side == 0:
        small[3, 0:F, :] = total
        left = jnp.sum(jnp.where(lanes == 0, s, 0.0), axis=1, keepdims=True)
        right = jnp.sum(jnp.where(lanes == EY - 1, s, 0.0), axis=1, keepdims=True)
        lam_edge = jnp.where(lanes == S_RIGHT, right, jnp.where(lanes == S_LEFT, left, lam_edge))
        small[4, 0:F, :] = u_edge
        small[5, 0:F, :] = lam_edge
        small[6, 0:F, :] = jnp.where(lanes < HALF, right, left)


def load_floors(side, mate, bottom_ref, floors):
    pick = bottom_ref[0, side].astype(F32)
    for group in range(1, bottom_ref.shape[0]):
        pick = jnp.where(mate == group, bottom_ref[group, side].astype(F32), pick)
    for k in range(NP * NP):
        floors[k, 0:BOTTOM, :] = pick[BOTTOM * k : BOTTOM * (k + 1)]


def outside(side, a, b, c, odd, first_ref, second_ref, floors):
    face = None
    if a in (0, 5):
        one, two = first_ref[side, b, c], second_ref[side, b, c]
        near = jnp.where(odd, one, two) if a == 0 else jnp.where(odd, two, one)
        face = near.astype(F32)
    if c == 5:
        row_ids = lax.broadcasted_iota(jnp.int32, (F, EY), 0)
        x = jnp.where(row_ids < BOTTOM, floors[a * NP + b], 0.0)
        face = x if face is None else face + x
    return face


def outer_kernel(
    first_ref, second_ref, bottom_ref, adj_ref, partner_hbm, owner_hbm, small_hbm,
    send_ref, mate_ref,
    floors, tile, partner_ref, owner_ref, small, sems,
):
    arrivals = [
        pltpu.make_async_copy(src, dst, sems.at[i])
        for i, (src, dst) in enumerate(
            ((small_hbm, small), (partner_hbm, partner_ref), (owner_hbm, owner_ref))
        )
    ]
    for copy in arrivals:
        copy.start()
    odd = lax.rem(lax.axis_index("gx"), 2) == 1
    total = jnp.zeros((F, EY), F32)
    for a in (0, 5):
        for b in range(NP):
            for c in range(5):
                face = outside(0, a, b, c, odd, first_ref, second_ref, floors)
                total = total + adj_ref[a, b, c].astype(F32) * face
    for copy in arrivals:
        copy.wait()
    mate = partner_ref[lax.axis_index("layer")]
    mate_ref[...] = mate
    load_floors(0, mate, bottom_ref, floors)
    for a in range(NP):
        for b in range(NP):
            face = outside(0, a, b, 5, odd, first_ref, second_ref, floors)
            total = total + adj_ref[a, b, 5].astype(F32) * face
    total = small[3, 0:F, :] + TAU * total
    total = DT * total
    high = total.astype(BF16)
    rest = total - high.astype(F32)
    middle = rest.astype(BF16)
    low = (rest - middle.astype(F32)).astype(BF16)
    owner = owner_ref[0]
    count = send_ref.shape[0]
    lane = lane_ids(1)
    own_left = jnp.sum(jnp.where(lane == 0, owner, 0), axis=1, keepdims=True).astype(F32)
    own_right = jnp.sum(jnp.where(lane == EY - 1, owner, 0), axis=1, keepdims=True).astype(F32)
    zeros = jnp.zeros((1, EY), F32)
    tile[...] = jnp.zeros_like(tile)
    for i in range(2):
        tile[0:F, :] = small[4 + i, 0:F, :]
        end = tile[...].astype(BF16)
        for target in range(count):
            send_ref[target, (2 + i) * ROWS : (3 + i) * ROWS, :] = end
    tile[F : F + 1, :] = zeros + own_left
    tile[F + 1 : F + 2, :] = zeros + own_right
    for target in range(count):
        cells = lax.broadcasted_iota(jnp.int32, (CELLS_DEV, EY), 0) + CELLS_DEV * target
        held = (cells == owner).astype(BF16)
        tile[0:F, :] = sum(
            lax.dot_general(x, held, (((1,), (1,)), ((), ())), preferred_element_type=F32)
            for x in (low, middle, high)
        )
        whole = tile[...]
        top = whole.astype(BF16)
        send_ref[target, 0:ROWS, :] = top
        send_ref[target, ROWS : 2 * ROWS, :] = (whole - top.astype(F32)).astype(BF16)


def last_kernel(
    got_ref, small, strip_ref, side_ref, top_ref, second_ref, first_ref, bottom_ref, mate_ref,
    wave_ref, adj_ref, old_wave_ref, old_adj_ref,
    new_wave_ref, new_adj_ref, cell_ref,
    patched, side_new, top_new, cell, floors, sems,
):
    me = lax.axis_index("gy")
    odd = lax.rem(lax.axis_index("gx"), 2) == 1
    mate = mate_ref[...]
    count = got_ref.shape[0]
    copies = []

    def send(src, dst):
        copies.append(pltpu.make_async_copy(src, dst, sems.at[len(copies)]))
        copies[-1].start()

    s = small[0, 0:F, :]
    factors = DT * s, DT

    def finished(side, a, b, c):
        rate = (side_ref[side, a // 5, b, c] if a in (0, 5) else top_ref[side, a - 1, b]).astype(F32)
        rate = rate + TAU * outside(side, a, b, c, odd, first_ref, second_ref, floors.at[side])
        return (adj_ref if side else wave_ref)[a, b, c].astype(F32) + factors[side] * rate

    for side, out_ref in ((0, new_wave_ref), (1, new_adj_ref)):
        load_floors(side, mate, bottom_ref, floors.at[side])
        for a in range(NP):
            for b in range(1, 5):
                if a in (0, 5):
                    for c in range(NP):
                        side_new[side, a // 5, b - 1, c] = finished(side, a, b, c).astype(BF16)
                else:
                    top_new[side, a - 1, b - 1] = finished(side, a, b, 5).astype(BF16)
            if a in (0, 5):
                send(side_new.at[side, a // 5], out_ref.at[a, 1:5])
        send(top_new.at[side], out_ref.at[1:5, 1:5, 5])
    lanes = lane_ids(F)
    upper = lanes >= HALF

    def tile(j, i):
        return got_ref[j, ROWS * i : ROWS * (i + 1), :].astype(F32)

    cells = jnp.zeros((F, EY), F32)
    lane = (lane_ids(1) + CELLS_DEV * me).astype(F32)
    for j in range(count):
        sums = tile(j, 0) + tile(j, 1)
        cells = cells + sums[0:F]
        lam = tile(j, 3)[0:F]
        for other, side, row in ((j - 1, upper, F), (j + 1, lanes < HALF, F + 1)):
            if 0 <= other < count:
                pairs = jnp.where(side, lam * tile(other, 2)[0:F], 0.0)
                value = (DT * TAU) * jnp.sum(pairs, axis=1, keepdims=True)
                cells = cells + jnp.where(sums[row : row + 1] == lane, value, 0.0)
    for f in range(F):
        cell[f] = cells[f : f + 1]
    send(cell, cell_ref)

    below = lax.max(me - 1, 0)
    above = lax.min(me + 1, count - 1)

    def held(values, column):
        return jnp.sum(jnp.where(lanes == column, values, 0.0), axis=1, keepdims=True)

    for side, out_ref in ((0, new_wave_ref), (1, new_adj_ref)):
        low = jnp.where(me > 0, tile(below, 2 + side)[0:F], 0.0)
        high = jnp.where(me < count - 1, tile(above, 2 + side)[0:F], 0.0)
        if side == 0:
            near = jnp.where(upper, low, high) * small[6, 0:F, :]
        else:
            near = jnp.where(upper, high * held(high, S_LEFT), low * held(low, S_RIGHT))
        near = (DT * TAU) * near
        edge = small[1 + side, 0:F, :] + near
        for b, end, start in ((0, 0, HALF if side == 0 else 0), (1, EY - 1, 0 if side == 0 else HALF)):
            for a in range(NP):
                for c in range(NP):
                    shift = (end - start - a * NP - c) % EY
                    if a in (0, 5) or c == 5:
                        old = finished(side, a, 5 * b, c)
                        moved = old + pltpu.roll(near, shift, 1)
                    else:
                        old = strip_ref[side, a - 1, b, c].astype(F32)
                        moved = pltpu.roll(edge, shift, 1)
                    patched[side, b, a, c] = jnp.where(lanes == end, moved, old).astype(BF16)
            send(patched.at[side, b], out_ref.at[:, 5 * b])
    for copy in copies:
        copy.wait()


def swap(x, axis, pairs):
    return lax.ppermute(x, axis, [(i, j) for i, j in pairs] + [(j, i) for i, j in pairs])


def per_device(wave, adjoint_source, coupling, stiffness, partner, owner):
    wave = wave[:, 0, 0].transpose(1, 2, 3, 0, 4)
    adj = adjoint_source[:, 0, 0].transpose(1, 2, 3, 0, 4)
    stiff = stiffness[:, 0]
    coup = coupling[0][:, :, None, :]
    own = owner[0]
    layers, columns, count = (lax.axis_size(axis) for axis in ("layer", "gx", "gy"))
    field = jax.ShapeDtypeStruct((NP, NP, NP, F, EY), BF16)
    faces = jax.ShapeDtypeStruct((2, NP, NP, F, EY), BF16)
    traces = jax.ShapeDtypeStruct((layers, 2, BOTTOM * NP * NP, EY), BF16)
    vmem = pl.BlockSpec(memory_space=pltpu.VMEM)
    hbm = pl.BlockSpec(memory_space=pltpu.HBM)
    params = pltpu.CompilerParams(vmem_limit_bytes=VMEM_LIMIT)

    def far(*arrays):
        return tuple(pltpu.with_memory_space_constraint(x, pltpu.HBM) for x in arrays)

    second, first, bottom = pl.pallas_call(
        prep_kernel,
        out_shape=(faces, faces, traces),
        in_specs=[hbm] * 3,
        out_specs=(hbm,) * 3,
        scratch_shapes=[
            pltpu.VMEM((2, NP, NP, F, EY), BF16),
            pltpu.VMEM((2, NP, NP, F, EY), BF16),
            pltpu.VMEM((2, NP, NP, F, EY), BF16),
            pltpu.VMEM((F, 1, EY), F32),
            pltpu.VMEM((ROWS, EY), F32),
            pltpu.VMEM((BOTTOM * NP * NP, EY), F32),
            pltpu.VMEM(traces.shape[1:], BF16),
            pltpu.SemaphoreType.DMA((11 + layers,)),
        ],
        compiler_params=params,
    )(*far(wave, adj, stiff))

    second = swap(second, "gx", [(i, i + 1) for i in range(1, columns - 1, 2)])
    first = swap(first, "gx", [(i, i + 1) for i in range(0, columns - 1, 2)])
    bottom = lax.all_to_all(bottom, "layer", 0, 0, tiled=True)

    side_shape, top_shape, strip_shape = (2, 2, NP, NP, F, EY), (2, 4, NP, F, EY), (2, 4, 2, 5, F, EY)
    small_shape = (7, ROWS, EY)
    new_wave, new_adj, sides, tops, strips, small = pl.pallas_call(
        inner_kernel,
        out_shape=(
            pltpu.HBM(field.shape, BF16),
            pltpu.HBM(field.shape, BF16),
            pltpu.HBM(side_shape, BF16),
            pltpu.HBM(top_shape, BF16),
            pltpu.HBM(strip_shape, BF16),
            pltpu.HBM(small_shape, F32),
        ),
        in_specs=[vmem] * 3 + [hbm],
        out_specs=(hbm,) * 6,
        scratch_shapes=[
            pltpu.VMEM((ROWS, EY), F32),
            pltpu.VMEM((3, ROWS, EY), F32),
            pltpu.VMEM((3, NP * ROWS, EY), BF16),
            pltpu.VMEM((2, NP, NP, NP, ROWS, EY), F32),
            pltpu.VMEM((2, NP, NP, NP, ROWS, EY), BF16),
            pltpu.VMEM((NP, NP, NP, ROWS, EY), F32),
            pltpu.VMEM((2, 4, 4, 5, F, EY), BF16),
            pltpu.VMEM(side_shape, BF16),
            pltpu.VMEM(top_shape, BF16),
            pltpu.VMEM(strip_shape, BF16),
            pltpu.VMEM(small_shape, F32),
            pltpu.VMEM(coup.shape, F32),
            pltpu.SemaphoreType.DMA((30,)),
        ],
        compiler_params=params,
        cost_estimate=pl.CostEstimate(flops=2**31, bytes_accessed=2**23, transcendentals=0),
    )(wave, adj, stiff, *far(coup))

    send, mate = pl.pallas_call(
        outer_kernel,
        out_shape=(
            jax.ShapeDtypeStruct((count, 4 * ROWS, EY), BF16),
            jax.ShapeDtypeStruct((1, EY), jnp.int32),
        ),
        in_specs=[vmem] * 4 + [hbm] * 3,
        out_specs=(vmem,) * 2,
        scratch_shapes=[
            pltpu.VMEM((NP * NP, F, EY), F32),
            pltpu.VMEM((ROWS, EY), F32),
            pltpu.VMEM(partner.shape, jnp.int32),
            pltpu.VMEM(own.shape, jnp.int32),
            pltpu.VMEM(small_shape, F32),
            pltpu.SemaphoreType.DMA((3,)),
        ],
        compiler_params=params,
    )(first, second, bottom, adj, *far(partner, own, small))

    got = lax.all_to_all(send, "gy", 0, 0, tiled=True)

    new_wave, new_adj, cells = pl.pallas_call(
        last_kernel,
        out_shape=(field, field, jax.ShapeDtypeStruct((F, 1, CELLS_DEV), F32)),
        in_specs=[vmem] * 11 + [hbm] * 2,
        out_specs=(hbm,) * 3,
        scratch_shapes=[
            pltpu.VMEM((2, 2, NP, NP, F, EY), BF16),
            pltpu.VMEM((2, 2, 4, NP, F, EY), BF16),
            pltpu.VMEM((2, 4, 4, F, EY), BF16),
            pltpu.VMEM((F, 1, CELLS_DEV), F32),
            pltpu.VMEM((2, NP * NP, F, EY), F32),
            pltpu.SemaphoreType.DMA((11,)),
        ],
        input_output_aliases={11: 0, 12: 1},
        compiler_params=params,
    )(got, small, strips, sides, tops, second, first, bottom, mate, wave, adj, new_wave, new_adj)

    new_wave = new_wave.transpose(3, 0, 1, 2, 4)[:, None, None]
    new_adj = new_adj.transpose(3, 0, 1, 2, 4)[:, None, None]
    return (new_wave, new_adj, cells.transpose(1, 0, 2)[None])


def solution(mesh):
    return jax.shard_map(
        per_device,
        mesh=mesh,
        in_specs=(
            P(None, "layer", "gx", None, None, None, "gy"),
            P(None, "layer", "gx", None, None, None, "gy"),
            P("layer", None, None, None),
            P(None, "layer", "gx", "gy"),
            P(None, "gx", "gy"),
            P("layer", "gx", "gy"),
        ),
        out_specs=(
            P(None, "layer", "gx", None, None, None, "gy"),
            P(None, "layer", "gx", None, None, None, "gy"),
            P("layer", "gx", None, "gy"),
        ),
        check_vma=False,
    )
```

```python
import functools
import math

import jax
import jax.numpy as jnp
import numpy as np
from jax import lax
from jax.experimental import pallas as pl
from jax.experimental.pallas import tpu as pltpu
from jax.sharding import PartitionSpec as P

F = 13
ROWS = 16
NP = 6
EY = 128
CELLS_DEV = 128
BOTTOM = 4
HALF = 64
S_RIGHT = 36
S_LEFT = 100
DT = 0.05
TAU = 7.5
F32 = jnp.float32
BF16 = jnp.bfloat16
VMEM_LIMIT = 40 * 1024 * 1024


def lobatto_derivative():
    outer = math.sqrt(1.0 / 3.0 + 2.0 * math.sqrt(7.0) / 21.0)
    inner = math.sqrt(1.0 / 3.0 - 2.0 * math.sqrt(7.0) / 21.0)
    nodes = np.array([-1.0, -outer, -inner, inner, outer, 1.0])
    weights = np.array(
        [
            1.0 / np.prod([nodes[col] - nodes[other] for other in range(6) if other != col])
            for col in range(6)
        ]
    )
    table = np.zeros((6, 6))
    for row_id in range(6):
        for col in range(6):
            if row_id != col:
                table[row_id, col] = weights[col] / weights[row_id] / (nodes[row_id] - nodes[col])
        table[row_id, row_id] = -np.sum(table[row_id])
    return table


def lane_ids(rows):
    return lax.broadcasted_iota(jnp.int32, (rows, EY), 1)


def load_scale(stiff_ref, scale):
    for f in range(F):
        scale[f : f + 1, :] = stiff_ref[f]
    return scale[0:F, :]


def prep_kernel(
    wave_ref, adj_ref, stiff_ref, second_ref, first_ref, bottom_ref,
    raw, kept, low, stiff, scale, rows, trace, sems,
):
    odd = lax.rem(lax.axis_index("gx"), 2)
    near = 5 * (1 - odd)
    far = 5 * odd
    copies = []

    def send(src, dst):
        copies.append(pltpu.make_async_copy(src, dst, sems.at[len(copies)]))
        copies[-1].start()
        return copies[-1]

    arrivals = [
        send(stiff_ref, stiff),
        send(adj_ref.at[:, :, 0], low.at[1]),
        send(wave_ref.at[:, :, 0], low.at[0]),
        send(adj_ref.at[far], raw.at[1]),
        send(adj_ref.at[near], raw.at[0]),
    ]
    arrivals += [send(wave_ref.at[far], kept.at[1]), send(wave_ref.at[near], kept.at[0])]
    leaving = []
    for copy in arrivals[0:3]:
        copy.wait()
    s = load_scale(stiff, scale)
    s4 = s[0:BOTTOM]
    for part in range(2):
        for a in range(NP):
            for b in range(NP):
                x = low[part, a, b].astype(F32)[0:BOTTOM]
                if part == 1:
                    x = x * s4
                k = BOTTOM * (a * NP + b)
                rows[k : k + BOTTOM, :] = x
        trace[part] = rows[...].astype(BF16)
    for group in range(bottom_ref.shape[0]):
        leaving.append(send(trace, bottom_ref.at[group]))
    for out_ref, at in ((second_ref, 1), (first_ref, 0)):
        arrivals[6 - at].wait()
        leaving.append(send(kept.at[at], out_ref.at[0]))
    for out_ref, at in ((second_ref, 1), (first_ref, 0)):
        arrivals[4 - at].wait()
        for b in range(NP):
            for c in range(NP):
                raw[at, b, c] = (raw[at, b, c].astype(F32) * s).astype(BF16)
        leaving.append(send(raw.at[at], out_ref.at[1]))
    for copy in leaving:
        copy.wait()


def build_matrices(side, coup_ref, cs, mats):
    table = lobatto_derivative()
    cs[...] = jnp.zeros_like(cs)
    for d in range(3):
        for f in range(F):
            cs[d, f : f + 1, 0:F] = coup_ref[d, f]
    block = lane_ids(ROWS) // ROWS
    spread = []
    for i in range(NP):
        row = jnp.zeros((ROWS, EY), F32)
        for k in range(NP):
            row = jnp.where(block == k, F32(table[i, k]), row)
        spread.append(row)
    for d in range(3):
        base = cs[d]
        if side == 1:
            base = -jnp.concatenate([base, jnp.zeros((EY - ROWS, EY), F32)], axis=0).T[0:ROWS]
        wide = base
        for k in range(1, NP):
            wide = wide + pltpu.roll(base, ROWS * k, 1)
        for i in range(NP):
            mats[d, ROWS * i : ROWS * (i + 1), :] = (wide * spread[i]).astype(BF16)


def put(edge, tile, frm, to):
    return jnp.where(lane_ids(F) == to, pltpu.roll(tile, (to - frm) % EY, 1), edge)


def inner_kernel(
    wave_ref, adj_ref, stiff_ref, coup_ref,
    new_wave_ref, new_adj_ref, side_out_ref, top_out_ref, strip_out_ref, small_out_ref,
    scale, cs, mats, padded, packed, acc, mid, side_ref, top_ref, strip_ref, small, coup, sems,
):
    copies = []

    def send(src, dst):
        copies.append(pltpu.make_async_copy(src, dst, sems.at[len(copies)]))
        copies[-1].start()
        return copies[-1]

    arrival = send(coup_ref, coup)
    s = load_scale(stiff_ref, scale)
    for a in range(NP):
        padded[:, a, :, :, 8:ROWS, :] = jnp.zeros((2, NP, NP, ROWS - 8, EY), F32)
        for b in range(NP):
            for c in range(NP):
                padded[0, a, b, c, 0:F, :] = wave_ref[a, b, c].astype(F32)
                padded[1, a, b, c, 0:F, :] = adj_ref[a, b, c].astype(F32) * s
        for side in range(2):
            packed[side, a] = padded[side, a].astype(BF16)
    arrival.wait()
    small[0, 0:F, :] = s

    def leave(side, a):
        out_ref = new_adj_ref if side else new_wave_ref
        if a in (0, 5):
            send(side_ref.at[side, a // 5], side_out_ref.at[side, a // 5])
        else:
            send(mid.at[side, a - 1], out_ref.at[a, 1:5, 0:5])
            send(top_ref.at[side, a - 1], top_out_ref.at[side, a - 1])
            send(strip_ref.at[side, a - 1], strip_out_ref.at[side, a - 1])

    for side in range(2):
        inner_side(
            side, adj_ref, s, coup, side_ref, top_ref, strip_ref, small,
            cs, mats, padded.at[side], packed.at[side], acc, mid, leave,
        )
    send(small, small_out_ref)
    for copy in copies[1:]:
        copy.wait()


def inner_side(
    side, adj_ref, s, coup_ref, side_ref, top_ref, strip_ref, small,
    cs, mats, padded, packed, acc, mid, leave,
):
    width = NP * ROWS
    lanes = lane_ids(F)
    row_ids = lax.broadcasted_iota(jnp.int32, (F, EY), 0)

    build_matrices(side, coup_ref, cs, mats)
    m = [mats[d][:, 0:width] for d in range(3)]
    for b in range(NP):
        right = jnp.concatenate([packed[:, b, c].reshape(width, EY) for c in range(NP)], axis=1)
        out = jnp.dot(m[0], right, preferred_element_type=F32)
        for c in range(NP):
            acc[:, b, c] = out[:, c * EY : (c + 1) * EY].reshape(NP, ROWS, EY)

    total = jnp.zeros((F, EY), F32)
    u_edge = jnp.zeros((F, EY), F32)
    lam_edge = jnp.zeros((F, EY), F32)
    edge = jnp.zeros((F, EY), F32)
    for a in range(NP):
        right = jnp.concatenate([packed[a, :, c].reshape(width, EY) for c in range(NP)], axis=1)
        along_b = jnp.dot(m[1], right, preferred_element_type=F32)
        right = jnp.concatenate([packed[a, b].reshape(width, EY) for b in range(NP)], axis=1)
        along_c = jnp.dot(m[2], right, preferred_element_type=F32)
        for b in range(NP):
            for c in range(NP):
                rate = (
                    acc[a, b, c]
                    + along_b[ROWS * b : ROWS * (b + 1), c * EY : (c + 1) * EY]
                    + along_c[ROWS * c : ROWS * (c + 1), b * EY : (b + 1) * EY]
                )[0:F]
                v = padded[a, b, c, 0:F, :]
                face = None
                own = (a in (0, 5)) + (b in (0, 5))
                if b == 0:
                    other = padded[a, 5, c, 0:F, :]
                    face = jnp.where(lanes == 0, 0.0, pltpu.roll(other, 1, 1))
                if b == 5:
                    other = padded[a, 0, c, 0:F, :]
                    face = jnp.where(lanes == EY - 1, 0.0, pltpu.roll(other, EY - 1, 1))
                if own:
                    rate = rate - (TAU * own) * v
                if face is not None:
                    rate = rate + TAU * face
                if c == 5:
                    rate = rate - jnp.where(row_ids < BOTTOM, TAU * v, 0.0)
                k = a * NP + c
                lam = adj_ref[a, b, c].astype(F32)
                if side == 0:
                    total = total + lam * rate
                    new = v + (DT * s) * rate
                else:
                    new = lam + DT * rate
                if a in (0, 5):
                    side_ref[side, a // 5, b, c] = rate.astype(BF16)
                elif c == 5:
                    top_ref[side, a - 1, b] = rate.astype(BF16)
                elif b in (0, 5):
                    strip_ref[side, a - 1, b // 5, c] = new.astype(BF16)
                else:
                    mid[side, a - 1, b - 1, c] = new.astype(BF16)
                if b == 0 and a not in (0, 5) and c != 5:
                    edge = put(edge, new, 0, HALF * (1 - side) + k)
                if b == 5 and a not in (0, 5) and c != 5:
                    edge = put(edge, new, EY - 1, HALF * side + k)
                if side == 0 and b == 0:
                    u_edge = put(u_edge, v, 0, k)
                    lam_edge = put(lam_edge, lam, 0, HALF + k)
                if side == 0 and b == 5:
                    u_edge = put(u_edge, v, EY - 1, HALF + k)
                    lam_edge = put(lam_edge, lam, EY - 1, k)
        leave(side, a)
    small[1 + side, 0:F, :] = edge
    if side == 0:
        small[3, 0:F, :] = total
        left = jnp.sum(jnp.where(lanes == 0, s, 0.0), axis=1, keepdims=True)
        right = jnp.sum(jnp.where(lanes == EY - 1, s, 0.0), axis=1, keepdims=True)
        lam_edge = jnp.where(lanes == S_RIGHT, right, jnp.where(lanes == S_LEFT, left, lam_edge))
        small[4, 0:F, :] = u_edge
        small[5, 0:F, :] = lam_edge
        small[6, 0:F, :] = jnp.where(lanes < HALF, right, left)


def load_floors(side, mate, bottom_ref, floors):
    pick = bottom_ref[0, side].astype(F32)
    for group in range(1, bottom_ref.shape[0]):
        pick = jnp.where(mate == group, bottom_ref[group, side].astype(F32), pick)
    for k in range(NP * NP):
        floors[k, 0:BOTTOM, :] = pick[BOTTOM * k : BOTTOM * (k + 1)]


def outside(side, a, b, c, odd, first_ref, second_ref, floors):
    face = None
    if a in (0, 5):
        one, two = first_ref[side, b, c], second_ref[side, b, c]
        near = jnp.where(odd, one, two) if a == 0 else jnp.where(odd, two, one)
        face = near.astype(F32)
    if c == 5:
        row_ids = lax.broadcasted_iota(jnp.int32, (F, EY), 0)
        x = jnp.where(row_ids < BOTTOM, floors[a * NP + b], 0.0)
        face = x if face is None else face + x
    return face


def trace_kernel(
    bottom_ref, adj_hbm, partner_hbm, owner_hbm, small_hbm,
    lam_side_ref, ends_ref, total_ref, owner_ref, mate_ref,
    floors, partner_ref, small, lam_top, tile, sems,
):
    copies = [
        pltpu.make_async_copy(src, dst, sems.at[i])
        for i, (src, dst) in enumerate(
            (
                (partner_hbm, partner_ref),
                (adj_hbm.at[:, :, 5], lam_top),
                (small_hbm, small),
                (owner_hbm, owner_ref),
                (adj_hbm.at[0], lam_side_ref.at[0]),
                (adj_hbm.at[5], lam_side_ref.at[1]),
            )
        )
    ]
    for copy in copies:
        copy.start()
    copies[0].wait()
    mate = partner_ref[lax.axis_index("layer")]
    mate_ref[...] = mate
    floors[...] = jnp.zeros_like(floors)
    load_floors(0, mate, bottom_ref, floors)
    copies[1].wait()
    total = jnp.zeros((F, EY), F32)
    row_ids = lax.broadcasted_iota(jnp.int32, (F, EY), 0)
    for a in range(NP):
        for b in range(NP):
            total = total + lam_top[a, b].astype(F32) * floors[a * NP + b]
    copies[2].wait()
    total_ref[...] = small[3, 0:F, :] + jnp.where(row_ids < BOTTOM, TAU * total, 0.0)
    tile[...] = jnp.zeros_like(tile)
    for i in range(2):
        tile[0:F, :] = small[4 + i, 0:F, :]
        ends_ref[i] = tile[...].astype(BF16)
    for copy in copies[3:]:
        copy.wait()


def outer_kernel(
    first_ref, second_ref, lam_side_ref, ends_ref, total_ref, owner_ref,
    send_ref,
    tile,
):
    odd = lax.rem(lax.axis_index("gx"), 2) == 1
    total = jnp.zeros((F, EY), F32)
    for b in range(NP):
        for c in range(NP):
            one, two = first_ref[0, b, c].astype(F32), second_ref[0, b, c].astype(F32)
            low, high = jnp.where(odd, one, two), jnp.where(odd, two, one)
            total = total + lam_side_ref[0, b, c].astype(F32) * low
            total = total + lam_side_ref[1, b, c].astype(F32) * high
    total = total_ref[...] + TAU * total
    total = DT * total
    high = total.astype(BF16)
    rest = total - high.astype(F32)
    middle = rest.astype(BF16)
    low = (rest - middle.astype(F32)).astype(BF16)
    owner = owner_ref[0]
    count = send_ref.shape[0]
    lane = lane_ids(1)
    own_left = jnp.sum(jnp.where(lane == 0, owner, 0), axis=1, keepdims=True).astype(F32)
    own_right = jnp.sum(jnp.where(lane == EY - 1, owner, 0), axis=1, keepdims=True).astype(F32)
    zeros = jnp.zeros((1, EY), F32)
    tile[...] = jnp.zeros_like(tile)
    for i in range(2):
        for target in range(count):
            send_ref[target, (2 + i) * ROWS : (3 + i) * ROWS, :] = ends_ref[i]
    tile[F : F + 1, :] = zeros + own_left
    tile[F + 1 : F + 2, :] = zeros + own_right
    for target in range(count):
        cells = lax.broadcasted_iota(jnp.int32, (CELLS_DEV, EY), 0) + CELLS_DEV * target
        held = (cells == owner).astype(BF16)
        tile[0:F, :] = sum(
            lax.dot_general(x, held, (((1,), (1,)), ((), ())), preferred_element_type=F32)
            for x in (low, middle, high)
        )
        whole = tile[...]
        top = whole.astype(BF16)
        send_ref[target, 0:ROWS, :] = top
        send_ref[target, ROWS : 2 * ROWS, :] = (whole - top.astype(F32)).astype(BF16)


def last_kernel(
    got_ref, small, strip_ref, side_ref, top_ref, second_ref, first_ref, bottom_ref, mate_ref,
    wave_ref, adj_ref, old_wave_ref, old_adj_ref,
    new_wave_ref, new_adj_ref, cell_ref,
    patched, side_new, top_new, cell, floors, sems,
):
    me = lax.axis_index("gy")
    odd = lax.rem(lax.axis_index("gx"), 2) == 1
    mate = mate_ref[...]
    count = got_ref.shape[0]
    copies = []

    def send(src, dst):
        copies.append(pltpu.make_async_copy(src, dst, sems.at[len(copies)]))
        copies[-1].start()

    s = small[0, 0:F, :]
    factors = DT * s, DT

    def finished(side, a, b, c):
        rate = (side_ref[side, a // 5, b, c] if a in (0, 5) else top_ref[side, a - 1, b]).astype(F32)
        rate = rate + TAU * outside(side, a, b, c, odd, first_ref, second_ref, floors.at[side])
        return (adj_ref if side else wave_ref)[a, b, c].astype(F32) + factors[side] * rate

    for side, out_ref in ((0, new_wave_ref), (1, new_adj_ref)):
        load_floors(side, mate, bottom_ref, floors.at[side])
        for a in range(NP):
            for b in range(1, 5):
                if a in (0, 5):
                    for c in range(NP):
                        side_new[side, a // 5, b - 1, c] = finished(side, a, b, c).astype(BF16)
                else:
                    top_new[side, a - 1, b - 1] = finished(side, a, b, 5).astype(BF16)
            if a in (0, 5):
                send(side_new.at[side, a // 5], out_ref.at[a, 1:5])
        send(top_new.at[side], out_ref.at[1:5, 1:5, 5])
    lanes = lane_ids(F)
    upper = lanes >= HALF

    def tile(j, i):
        return got_ref[j, ROWS * i : ROWS * (i + 1), :].astype(F32)

    cells = jnp.zeros((F, EY), F32)
    lane = (lane_ids(1) + CELLS_DEV * me).astype(F32)
    for j in range(count):
        sums = tile(j, 0) + tile(j, 1)
        cells = cells + sums[0:F]
        lam = tile(j, 3)[0:F]
        for other, side, row in ((j - 1, upper, F), (j + 1, lanes < HALF, F + 1)):
            if 0 <= other < count:
                pairs = jnp.where(side, lam * tile(other, 2)[0:F], 0.0)
                value = (DT * TAU) * jnp.sum(pairs, axis=1, keepdims=True)
                cells = cells + jnp.where(sums[row : row + 1] == lane, value, 0.0)
    for f in range(F):
        cell[f] = cells[f : f + 1]
    send(cell, cell_ref)

    below = lax.max(me - 1, 0)
    above = lax.min(me + 1, count - 1)

    def held(values, column):
        return jnp.sum(jnp.where(lanes == column, values, 0.0), axis=1, keepdims=True)

    for side, out_ref in ((0, new_wave_ref), (1, new_adj_ref)):
        low = jnp.where(me > 0, tile(below, 2 + side)[0:F], 0.0)
        high = jnp.where(me < count - 1, tile(above, 2 + side)[0:F], 0.0)
        if side == 0:
            near = jnp.where(upper, low, high) * small[6, 0:F, :]
        else:
            near = jnp.where(upper, high * held(high, S_LEFT), low * held(low, S_RIGHT))
        near = (DT * TAU) * near
        edge = small[1 + side, 0:F, :] + near
        for b, end, start in ((0, 0, HALF if side == 0 else 0), (1, EY - 1, 0 if side == 0 else HALF)):
            for a in range(NP):
                for c in range(NP):
                    shift = (end - start - a * NP - c) % EY
                    if a in (0, 5) or c == 5:
                        old = finished(side, a, 5 * b, c)
                        moved = old + pltpu.roll(near, shift, 1)
                    else:
                        old = strip_ref[side, a - 1, b, c].astype(F32)
                        moved = pltpu.roll(edge, shift, 1)
                    patched[side, b, a, c] = jnp.where(lanes == end, moved, old).astype(BF16)
            send(patched.at[side, b], out_ref.at[:, 5 * b])
    for copy in copies:
        copy.wait()


def swap(x, axis, pairs):
    return lax.ppermute(x, axis, [(i, j) for i, j in pairs] + [(j, i) for i, j in pairs])


def per_device(wave, adjoint_source, coupling, stiffness, partner, owner):
    wave = wave[:, 0, 0].transpose(1, 2, 3, 0, 4)
    adj = adjoint_source[:, 0, 0].transpose(1, 2, 3, 0, 4)
    stiff = stiffness[:, 0]
    coup = coupling[0][:, :, None, :]
    own = owner[0]
    layers, columns, count = (lax.axis_size(axis) for axis in ("layer", "gx", "gy"))
    field = jax.ShapeDtypeStruct((NP, NP, NP, F, EY), BF16)
    faces = jax.ShapeDtypeStruct((2, NP, NP, F, EY), BF16)
    traces = jax.ShapeDtypeStruct((layers, 2, BOTTOM * NP * NP, EY), BF16)
    vmem = pl.BlockSpec(memory_space=pltpu.VMEM)
    hbm = pl.BlockSpec(memory_space=pltpu.HBM)
    params = pltpu.CompilerParams(vmem_limit_bytes=VMEM_LIMIT)

    def far(*arrays):
        return tuple(pltpu.with_memory_space_constraint(x, pltpu.HBM) for x in arrays)

    second, first, bottom = pl.pallas_call(
        prep_kernel,
        out_shape=(faces, faces, traces),
        in_specs=[hbm] * 3,
        out_specs=(hbm,) * 3,
        scratch_shapes=[
            pltpu.VMEM((2, NP, NP, F, EY), BF16),
            pltpu.VMEM((2, NP, NP, F, EY), BF16),
            pltpu.VMEM((2, NP, NP, F, EY), BF16),
            pltpu.VMEM((F, 1, EY), F32),
            pltpu.VMEM((ROWS, EY), F32),
            pltpu.VMEM((BOTTOM * NP * NP, EY), F32),
            pltpu.VMEM(traces.shape[1:], BF16),
            pltpu.SemaphoreType.DMA((11 + layers,)),
        ],
        compiler_params=params,
    )(*far(wave, adj, stiff))

    second = swap(second, "gx", [(i, i + 1) for i in range(1, columns - 1, 2)])
    first = swap(first, "gx", [(i, i + 1) for i in range(0, columns - 1, 2)])
    bottom = lax.all_to_all(bottom, "layer", 0, 0, tiled=True)

    side_shape, top_shape, strip_shape = (2, 2, NP, NP, F, EY), (2, 4, NP, F, EY), (2, 4, 2, 5, F, EY)
    small_shape = (7, ROWS, EY)
    new_wave, new_adj, sides, tops, strips, small = pl.pallas_call(
        inner_kernel,
        out_shape=(
            pltpu.HBM(field.shape, BF16),
            pltpu.HBM(field.shape, BF16),
            pltpu.HBM(side_shape, BF16),
            pltpu.HBM(top_shape, BF16),
            pltpu.HBM(strip_shape, BF16),
            pltpu.HBM(small_shape, F32),
        ),
        in_specs=[vmem] * 3 + [hbm],
        out_specs=(hbm,) * 6,
        scratch_shapes=[
            pltpu.VMEM((ROWS, EY), F32),
            pltpu.VMEM((3, ROWS, EY), F32),
            pltpu.VMEM((3, NP * ROWS, EY), BF16),
            pltpu.VMEM((2, NP, NP, NP, ROWS, EY), F32),
            pltpu.VMEM((2, NP, NP, NP, ROWS, EY), BF16),
            pltpu.VMEM((NP, NP, NP, ROWS, EY), F32),
            pltpu.VMEM((2, 4, 4, 5, F, EY), BF16),
            pltpu.VMEM(side_shape, BF16),
            pltpu.VMEM(top_shape, BF16),
            pltpu.VMEM(strip_shape, BF16),
            pltpu.VMEM(small_shape, F32),
            pltpu.VMEM(coup.shape, F32),
            pltpu.SemaphoreType.DMA((30,)),
        ],
        compiler_params=params,
        cost_estimate=pl.CostEstimate(flops=2**31, bytes_accessed=2**23, transcendentals=0),
    )(wave, adj, stiff, *far(coup))

    lam_sides, ends, total, own, mate = pl.pallas_call(
        trace_kernel,
        out_shape=(
            jax.ShapeDtypeStruct(side_shape[1:], BF16),
            jax.ShapeDtypeStruct((2, ROWS, EY), BF16),
            jax.ShapeDtypeStruct((F, EY), F32),
            jax.ShapeDtypeStruct((1, EY), jnp.int32),
            jax.ShapeDtypeStruct((1, EY), jnp.int32),
        ),
        in_specs=[vmem] + [hbm] * 4,
        out_specs=(vmem,) * 5,
        scratch_shapes=[
            pltpu.VMEM((NP * NP, F, EY), F32),
            pltpu.VMEM(partner.shape, jnp.int32),
            pltpu.VMEM(small_shape, F32),
            pltpu.VMEM((NP, NP, F, EY), BF16),
            pltpu.VMEM((ROWS, EY), F32),
            pltpu.SemaphoreType.DMA((6,)),
        ],
        compiler_params=params,
        cost_estimate=pl.CostEstimate(flops=2**29, bytes_accessed=2**22, transcendentals=0),
    )(bottom, *far(adj, partner, own, small))

    send = pl.pallas_call(
        outer_kernel,
        out_shape=jax.ShapeDtypeStruct((count, 4 * ROWS, EY), BF16),
        in_specs=[vmem] * 6,
        out_specs=vmem,
        scratch_shapes=[pltpu.VMEM((ROWS, EY), F32)],
        compiler_params=params,
    )(first, second, lam_sides, ends, total, own)

    got = lax.all_to_all(send, "gy", 0, 0, tiled=True)

    new_wave, new_adj, cells = pl.pallas_call(
        last_kernel,
        out_shape=(field, field, jax.ShapeDtypeStruct((F, 1, CELLS_DEV), F32)),
        in_specs=[vmem] * 11 + [hbm] * 2,
        out_specs=(hbm,) * 3,
        scratch_shapes=[
            pltpu.VMEM((2, 2, NP, NP, F, EY), BF16),
            pltpu.VMEM((2, 2, 4, NP, F, EY), BF16),
            pltpu.VMEM((2, 4, 4, F, EY), BF16),
            pltpu.VMEM((F, 1, CELLS_DEV), F32),
            pltpu.VMEM((2, NP * NP, F, EY), F32),
            pltpu.SemaphoreType.DMA((11,)),
        ],
        input_output_aliases={11: 0, 12: 1},
        compiler_params=params,
    )(got, small, strips, sides, tops, second, first, bottom, mate, wave, adj, new_wave, new_adj)

    new_wave = new_wave.transpose(3, 0, 1, 2, 4)[:, None, None]
    new_adj = new_adj.transpose(3, 0, 1, 2, 4)[:, None, None]
    return (new_wave, new_adj, cells.transpose(1, 0, 2)[None])


def solution(mesh):
    return jax.shard_map(
        per_device,
        mesh=mesh,
        in_specs=(
            P(None, "layer", "gx", None, None, None, "gy"),
            P(None, "layer", "gx", None, None, None, "gy"),
            P("layer", None, None, None),
            P(None, "layer", "gx", "gy"),
            P(None, "gx", "gy"),
            P("layer", "gx", "gy"),
        ),
        out_specs=(
            P(None, "layer", "gx", None, None, None, "gy"),
            P(None, "layer", "gx", None, None, None, "gy"),
            P("layer", "gx", None, "gy"),
        ),
        check_vma=False,
    )
```

```python
import functools
import math

import jax
import jax.numpy as jnp
import numpy as np
from jax import lax
from jax.experimental import pallas as pl
from jax.experimental.pallas import tpu as pltpu
from jax.sharding import PartitionSpec as P

F = 13
ROWS = 16
NP = 6
EY = 128
CELLS_DEV = 128
BOTTOM = 4
HALF = 64
S_RIGHT = 36
S_LEFT = 100
DT = 0.05
TAU = 7.5
F32 = jnp.float32
BF16 = jnp.bfloat16
VMEM_LIMIT = 40 * 1024 * 1024


def lobatto_derivative():
    outer = math.sqrt(1.0 / 3.0 + 2.0 * math.sqrt(7.0) / 21.0)
    inner = math.sqrt(1.0 / 3.0 - 2.0 * math.sqrt(7.0) / 21.0)
    nodes = np.array([-1.0, -outer, -inner, inner, outer, 1.0])
    weights = np.array(
        [
            1.0 / np.prod([nodes[col] - nodes[other] for other in range(6) if other != col])
            for col in range(6)
        ]
    )
    table = np.zeros((6, 6))
    for row_id in range(6):
        for col in range(6):
            if row_id != col:
                table[row_id, col] = weights[col] / weights[row_id] / (nodes[row_id] - nodes[col])
        table[row_id, row_id] = -np.sum(table[row_id])
    return table


def lane_ids(rows):
    return lax.broadcasted_iota(jnp.int32, (rows, EY), 1)


def load_scale(stiff_ref, scale):
    for f in range(F):
        scale[f : f + 1, :] = stiff_ref[f]
    return scale[0:F, :]


def prep_kernel(
    wave_ref, adj_ref, stiff_ref, second_ref, first_ref, bottom_ref,
    raw, low, stiff, scale, rows, trace, sems,
):
    odd = lax.rem(lax.axis_index("gx"), 2)
    near = 5 * (1 - odd)
    far = 5 * odd
    copies = []

    def send(src, dst):
        copies.append(pltpu.make_async_copy(src, dst, sems.at[len(copies)]))
        copies[-1].start()
        return copies[-1]

    arrivals = [
        send(stiff_ref, stiff),
        send(adj_ref.at[:, :, 0], low.at[1]),
        send(wave_ref.at[:, :, 0], low.at[0]),
        send(adj_ref.at[far], raw.at[1]),
        send(adj_ref.at[near], raw.at[0]),
    ]
    leaving = [send(wave_ref.at[far], second_ref.at[0]), send(wave_ref.at[near], first_ref.at[0])]
    for copy in arrivals[0:3]:
        copy.wait()
    s = load_scale(stiff, scale)
    s4 = s[0:BOTTOM]
    for part in range(2):
        for a in range(NP):
            for b in range(NP):
                x = low[part, a, b].astype(F32)[0:BOTTOM]
                if part == 1:
                    x = x * s4
                k = BOTTOM * (a * NP + b)
                rows[k : k + BOTTOM, :] = x
        trace[part] = rows[...].astype(BF16)
    for group in range(bottom_ref.shape[0]):
        leaving.append(send(trace, bottom_ref.at[group]))
    for out_ref, at in ((second_ref, 1), (first_ref, 0)):
        arrivals[4 - at].wait()
        for b in range(NP):
            for c in range(NP):
                raw[at, b, c] = (raw[at, b, c].astype(F32) * s).astype(BF16)
        leaving.append(send(raw.at[at], out_ref.at[1]))
    for copy in leaving:
        copy.wait()


def build_matrices(side, coup_ref, cs, mats):
    table = lobatto_derivative()
    cs[...] = jnp.zeros_like(cs)
    for d in range(3):
        for f in range(F):
            cs[d, f : f + 1, 0:F] = coup_ref[d, f]
    block = lane_ids(ROWS) // ROWS
    spread = []
    for i in range(NP):
        row = jnp.zeros((ROWS, EY), F32)
        for k in range(NP):
            row = jnp.where(block == k, F32(table[i, k]), row)
        spread.append(row)
    for d in range(3):
        base = cs[d]
        if side == 1:
            base = -jnp.concatenate([base, jnp.zeros((EY - ROWS, EY), F32)], axis=0).T[0:ROWS]
        wide = base
        for k in range(1, NP):
            wide = wide + pltpu.roll(base, ROWS * k, 1)
        for i in range(NP):
            mats[d, ROWS * i : ROWS * (i + 1), :] = (wide * spread[i]).astype(BF16)


def put(edge, tile, frm, to):
    return jnp.where(lane_ids(F) == to, pltpu.roll(tile, (to - frm) % EY, 1), edge)


def inner_kernel(
    wave_ref, adj_ref, stiff_ref, coup_ref,
    new_wave_ref, new_adj_ref, side_out_ref, top_out_ref, strip_out_ref, small_out_ref,
    scale, cs, mats, padded, packed, acc, mid, side_ref, top_ref, strip_ref, small, coup, sems,
):
    copies = []

    def send(src, dst):
        copies.append(pltpu.make_async_copy(src, dst, sems.at[len(copies)]))
        copies[-1].start()
        return copies[-1]

    arrival = send(coup_ref, coup)
    s = load_scale(stiff_ref, scale)
    for a in range(NP):
        padded[:, a, :, :, 8:ROWS, :] = jnp.zeros((2, NP, NP, ROWS - 8, EY), F32)
        for b in range(NP):
            for c in range(NP):
                padded[0, a, b, c, 0:F, :] = wave_ref[a, b, c].astype(F32)
                padded[1, a, b, c, 0:F, :] = adj_ref[a, b, c].astype(F32) * s
        for side in range(2):
            packed[side, a] = padded[side, a].astype(BF16)
    arrival.wait()
    small[0, 0:F, :] = s

    def leave(side, a):
        out_ref = new_adj_ref if side else new_wave_ref
        if a in (0, 5):
            send(side_ref.at[side, a // 5], side_out_ref.at[side, a // 5])
        else:
            send(mid.at[side, a - 1], out_ref.at[a, 1:5, 0:5])
            send(top_ref.at[side, a - 1], top_out_ref.at[side, a - 1])
            send(strip_ref.at[side, a - 1], strip_out_ref.at[side, a - 1])

    for side in range(2):
        inner_side(
            side, adj_ref, s, coup, side_ref, top_ref, strip_ref, small,
            cs, mats, padded.at[side], packed.at[side], acc, mid, leave,
        )
    send(small, small_out_ref)
    for copy in copies[1:]:
        copy.wait()


def inner_side(
    side, adj_ref, s, coup_ref, side_ref, top_ref, strip_ref, small,
    cs, mats, padded, packed, acc, mid, leave,
):
    width = NP * ROWS
    lanes = lane_ids(F)
    row_ids = lax.broadcasted_iota(jnp.int32, (F, EY), 0)

    build_matrices(side, coup_ref, cs, mats)
    m = [mats[d][:, 0:width] for d in range(3)]
    for b in range(NP):
        right = jnp.concatenate([packed[:, b, c].reshape(width, EY) for c in range(NP)], axis=1)
        out = jnp.dot(m[0], right, preferred_element_type=F32)
        for c in range(NP):
            acc[:, b, c] = out[:, c * EY : (c + 1) * EY].reshape(NP, ROWS, EY)

    total = jnp.zeros((F, EY), F32)
    u_edge = jnp.zeros((F, EY), F32)
    lam_edge = jnp.zeros((F, EY), F32)
    edge = jnp.zeros((F, EY), F32)
    for a in range(NP):
        right = jnp.concatenate([packed[a, :, c].reshape(width, EY) for c in range(NP)], axis=1)
        along_b = jnp.dot(m[1], right, preferred_element_type=F32)
        right = jnp.concatenate([packed[a, b].reshape(width, EY) for b in range(NP)], axis=1)
        along_c = jnp.dot(m[2], right, preferred_element_type=F32)
        for b in range(NP):
            for c in range(NP):
                rate = (
                    acc[a, b, c]
                    + along_b[ROWS * b : ROWS * (b + 1), c * EY : (c + 1) * EY]
                    + along_c[ROWS * c : ROWS * (c + 1), b * EY : (b + 1) * EY]
                )[0:F]
                v = padded[a, b, c, 0:F, :]
                face = None
                own = (a in (0, 5)) + (b in (0, 5))
                if b == 0:
                    other = padded[a, 5, c, 0:F, :]
                    face = jnp.where(lanes == 0, 0.0, pltpu.roll(other, 1, 1))
                if b == 5:
                    other = padded[a, 0, c, 0:F, :]
                    face = jnp.where(lanes == EY - 1, 0.0, pltpu.roll(other, EY - 1, 1))
                if own:
                    rate = rate - (TAU * own) * v
                if face is not None:
                    rate = rate + TAU * face
                if c == 5:
                    rate = rate - jnp.where(row_ids < BOTTOM, TAU * v, 0.0)
                k = a * NP + c
                lam = adj_ref[a, b, c].astype(F32)
                if side == 0:
                    total = total + lam * rate
                    new = v + (DT * s) * rate
                else:
                    new = lam + DT * rate
                if a in (0, 5):
                    side_ref[side, a // 5, b, c] = rate.astype(BF16)
                elif c == 5:
                    top_ref[side, a - 1, b] = rate.astype(BF16)
                elif b in (0, 5):
                    strip_ref[side, a - 1, b // 5, c] = new.astype(BF16)
                else:
                    mid[side, a - 1, b - 1, c] = new.astype(BF16)
                if b == 0 and a not in (0, 5) and c != 5:
                    edge = put(edge, new, 0, HALF * (1 - side) + k)
                if b == 5 and a not in (0, 5) and c != 5:
                    edge = put(edge, new, EY - 1, HALF * side + k)
                if side == 0 and b == 0:
                    u_edge = put(u_edge, v, 0, k)
                    lam_edge = put(lam_edge, lam, 0, HALF + k)
                if side == 0 and b == 5:
                    u_edge = put(u_edge, v, EY - 1, HALF + k)
                    lam_edge = put(lam_edge, lam, EY - 1, k)
        leave(side, a)
    small[1 + side, 0:F, :] = edge
    if side == 0:
        small[3, 0:F, :] = total
        left = jnp.sum(jnp.where(lanes == 0, s, 0.0), axis=1, keepdims=True)
        right = jnp.sum(jnp.where(lanes == EY - 1, s, 0.0), axis=1, keepdims=True)
        lam_edge = jnp.where(lanes == S_RIGHT, right, jnp.where(lanes == S_LEFT, left, lam_edge))
        small[4, 0:F, :] = u_edge
        small[5, 0:F, :] = lam_edge
        small[6, 0:F, :] = jnp.where(lanes < HALF, right, left)


def load_floors(side, mate, bottom_ref, floors):
    pick = bottom_ref[0, side].astype(F32)
    for group in range(1, bottom_ref.shape[0]):
        pick = jnp.where(mate == group, bottom_ref[group, side].astype(F32), pick)
    for k in range(NP * NP):
        floors[k, 0:BOTTOM, :] = pick[BOTTOM * k : BOTTOM * (k + 1)]


def outside(side, a, b, c, odd, first_ref, second_ref, floors):
    face = None
    if a in (0, 5):
        one, two = first_ref[side, b, c], second_ref[side, b, c]
        near = jnp.where(odd, one, two) if a == 0 else jnp.where(odd, two, one)
        face = near.astype(F32)
    if c == 5:
        row_ids = lax.broadcasted_iota(jnp.int32, (F, EY), 0)
        x = jnp.where(row_ids < BOTTOM, floors[a * NP + b], 0.0)
        face = x if face is None else face + x
    return face


def trace_kernel(
    bottom_ref, adj_hbm, partner_hbm, owner_hbm, small_hbm,
    lam_side_ref, lam_top, ends_ref, total_ref, owner_ref, mate_ref,
    floors, partner_ref, small, tile, sems,
):
    copies = [
        pltpu.make_async_copy(src, dst, sems.at[i])
        for i, (src, dst) in enumerate(
            (
                (partner_hbm, partner_ref),
                (adj_hbm.at[:, :, 5], lam_top),
                (small_hbm, small),
                (owner_hbm, owner_ref),
                (adj_hbm.at[0], lam_side_ref.at[0]),
                (adj_hbm.at[5], lam_side_ref.at[1]),
            )
        )
    ]
    for copy in copies:
        copy.start()
    copies[0].wait()
    mate = partner_ref[lax.axis_index("layer")]
    mate_ref[...] = mate
    floors[...] = jnp.zeros_like(floors)
    load_floors(0, mate, bottom_ref, floors)
    copies[1].wait()
    total = jnp.zeros((F, EY), F32)
    row_ids = lax.broadcasted_iota(jnp.int32, (F, EY), 0)
    for a in range(NP):
        for b in range(NP):
            total = total + lam_top[a, b].astype(F32) * floors[a * NP + b]
    copies[2].wait()
    total_ref[...] = small[3, 0:F, :] + jnp.where(row_ids < BOTTOM, TAU * total, 0.0)
    tile[...] = jnp.zeros_like(tile)
    for i in range(2):
        tile[0:F, :] = small[4 + i, 0:F, :]
        ends_ref[i] = tile[...].astype(BF16)
    for copy in copies[3:]:
        copy.wait()


def outer_kernel(
    first_ref, second_ref, lam_side_ref, ends_ref, total_ref, owner_ref,
    send_ref,
    tile,
):
    odd = lax.rem(lax.axis_index("gx"), 2) == 1
    total = jnp.zeros((F, EY), F32)
    for b in range(NP):
        for c in range(NP):
            one, two = first_ref[0, b, c].astype(F32), second_ref[0, b, c].astype(F32)
            low, high = jnp.where(odd, one, two), jnp.where(odd, two, one)
            total = total + lam_side_ref[0, b, c].astype(F32) * low
            total = total + lam_side_ref[1, b, c].astype(F32) * high
    total = total_ref[...] + TAU * total
    total = DT * total
    high = total.astype(BF16)
    rest = total - high.astype(F32)
    middle = rest.astype(BF16)
    low = (rest - middle.astype(F32)).astype(BF16)
    owner = owner_ref[0]
    count = send_ref.shape[0]
    lane = lane_ids(1)
    own_left = jnp.sum(jnp.where(lane == 0, owner, 0), axis=1, keepdims=True).astype(F32)
    own_right = jnp.sum(jnp.where(lane == EY - 1, owner, 0), axis=1, keepdims=True).astype(F32)
    zeros = jnp.zeros((1, EY), F32)
    tile[...] = jnp.zeros_like(tile)
    for i in range(2):
        for target in range(count):
            send_ref[target, (2 + i) * ROWS : (3 + i) * ROWS, :] = ends_ref[i]
    tile[F : F + 1, :] = zeros + own_left
    tile[F + 1 : F + 2, :] = zeros + own_right
    for target in range(count):
        cells = lax.broadcasted_iota(jnp.int32, (CELLS_DEV, EY), 0) + CELLS_DEV * target
        held = (cells == owner).astype(BF16)
        tile[0:F, :] = sum(
            lax.dot_general(x, held, (((1,), (1,)), ((), ())), preferred_element_type=F32)
            for x in (low, middle, high)
        )
        whole = tile[...]
        top = whole.astype(BF16)
        send_ref[target, 0:ROWS, :] = top
        send_ref[target, ROWS : 2 * ROWS, :] = (whole - top.astype(F32)).astype(BF16)


def last_kernel(
    got_ref, small, strip_ref, side_ref, top_ref, second_ref, first_ref, bottom_ref, mate_ref,
    wave_ref, lam_side_ref, lam_top_ref, old_wave_ref, old_adj_ref,
    new_wave_ref, new_adj_ref, cell_ref,
    patched, side_new, top_new, cell, floors, sems,
):
    me = lax.axis_index("gy")
    odd = lax.rem(lax.axis_index("gx"), 2) == 1
    mate = mate_ref[...]
    count = got_ref.shape[0]
    copies = []

    def send(src, dst):
        copies.append(pltpu.make_async_copy(src, dst, sems.at[len(copies)]))
        copies[-1].start()

    s = small[0, 0:F, :]
    factors = DT * s, DT

    def finished(side, a, b, c):
        rate = (side_ref[side, a // 5, b, c] if a in (0, 5) else top_ref[side, a - 1, b]).astype(F32)
        rate = rate + TAU * outside(side, a, b, c, odd, first_ref, second_ref, floors.at[side])
        if side == 0:
            old = wave_ref[a, b, c]
        else:
            old = lam_side_ref[a // 5, b, c] if a in (0, 5) else lam_top_ref[a, b]
        return old.astype(F32) + factors[side] * rate

    for side, out_ref in ((0, new_wave_ref), (1, new_adj_ref)):
        load_floors(side, mate, bottom_ref, floors.at[side])
        for a in range(NP):
            for b in range(1, 5):
                if a in (0, 5):
                    for c in range(NP):
                        side_new[side, a // 5, b - 1, c] = finished(side, a, b, c).astype(BF16)
                else:
                    top_new[side, a - 1, b - 1] = finished(side, a, b, 5).astype(BF16)
            if a in (0, 5):
                send(side_new.at[side, a // 5], out_ref.at[a, 1:5])
        send(top_new.at[side], out_ref.at[1:5, 1:5, 5])
    lanes = lane_ids(F)
    upper = lanes >= HALF

    def tile(j, i):
        return got_ref[j, ROWS * i : ROWS * (i + 1), :].astype(F32)

    cells = jnp.zeros((F, EY), F32)
    lane = (lane_ids(1) + CELLS_DEV * me).astype(F32)
    for j in range(count):
        sums = tile(j, 0) + tile(j, 1)
        cells = cells + sums[0:F]
        lam = tile(j, 3)[0:F]
        for other, side, row in ((j - 1, upper, F), (j + 1, lanes < HALF, F + 1)):
            if 0 <= other < count:
                pairs = jnp.where(side, lam * tile(other, 2)[0:F], 0.0)
                value = (DT * TAU) * jnp.sum(pairs, axis=1, keepdims=True)
                cells = cells + jnp.where(sums[row : row + 1] == lane, value, 0.0)
    for f in range(F):
        cell[f] = cells[f : f + 1]
    send(cell, cell_ref)

    below = lax.max(me - 1, 0)
    above = lax.min(me + 1, count - 1)

    def held(values, column):
        return jnp.sum(jnp.where(lanes == column, values, 0.0), axis=1, keepdims=True)

    for side, out_ref in ((0, new_wave_ref), (1, new_adj_ref)):
        low = jnp.where(me > 0, tile(below, 2 + side)[0:F], 0.0)
        high = jnp.where(me < count - 1, tile(above, 2 + side)[0:F], 0.0)
        if side == 0:
            near = jnp.where(upper, low, high) * small[6, 0:F, :]
        else:
            near = jnp.where(upper, high * held(high, S_LEFT), low * held(low, S_RIGHT))
        near = (DT * TAU) * near
        edge = small[1 + side, 0:F, :] + near
        for b, end, start in ((0, 0, HALF if side == 0 else 0), (1, EY - 1, 0 if side == 0 else HALF)):
            for a in range(NP):
                for c in range(NP):
                    shift = (end - start - a * NP - c) % EY
                    if a in (0, 5) or c == 5:
                        old = finished(side, a, 5 * b, c)
                        moved = old + pltpu.roll(near, shift, 1)
                    else:
                        old = strip_ref[side, a - 1, b, c].astype(F32)
                        moved = pltpu.roll(edge, shift, 1)
                    patched[side, b, a, c] = jnp.where(lanes == end, moved, old).astype(BF16)
            send(patched.at[side, b], out_ref.at[:, 5 * b])
    for copy in copies:
        copy.wait()


def swap(x, axis, pairs):
    return lax.ppermute(x, axis, [(i, j) for i, j in pairs] + [(j, i) for i, j in pairs])


def per_device(wave, adjoint_source, coupling, stiffness, partner, owner):
    wave = wave[:, 0, 0].transpose(1, 2, 3, 0, 4)
    adj = adjoint_source[:, 0, 0].transpose(1, 2, 3, 0, 4)
    stiff = stiffness[:, 0]
    coup = coupling[0][:, :, None, :]
    own = owner[0]
    layers, columns, count = (lax.axis_size(axis) for axis in ("layer", "gx", "gy"))
    field = jax.ShapeDtypeStruct((NP, NP, NP, F, EY), BF16)
    faces = jax.ShapeDtypeStruct((2, NP, NP, F, EY), BF16)
    traces = jax.ShapeDtypeStruct((layers, 2, BOTTOM * NP * NP, EY), BF16)
    vmem = pl.BlockSpec(memory_space=pltpu.VMEM)
    hbm = pl.BlockSpec(memory_space=pltpu.HBM)
    params = pltpu.CompilerParams(vmem_limit_bytes=VMEM_LIMIT)

    def far(*arrays):
        return tuple(pltpu.with_memory_space_constraint(x, pltpu.HBM) for x in arrays)

    second, first, bottom = pl.pallas_call(
        prep_kernel,
        out_shape=(faces, faces, traces),
        in_specs=[hbm] * 3,
        out_specs=(hbm,) * 3,
        scratch_shapes=[
            pltpu.VMEM((2, NP, NP, F, EY), BF16),
            pltpu.VMEM((2, NP, NP, F, EY), BF16),
            pltpu.VMEM((F, 1, EY), F32),
            pltpu.VMEM((ROWS, EY), F32),
            pltpu.VMEM((BOTTOM * NP * NP, EY), F32),
            pltpu.VMEM(traces.shape[1:], BF16),
            pltpu.SemaphoreType.DMA((9 + layers,)),
        ],
        compiler_params=params,
    )(*far(wave, adj, stiff))

    second = swap(second, "gx", [(i, i + 1) for i in range(1, columns - 1, 2)])
    first = swap(first, "gx", [(i, i + 1) for i in range(0, columns - 1, 2)])
    bottom = lax.all_to_all(bottom, "layer", 0, 0, tiled=True)

    side_shape, top_shape, strip_shape = (2, 2, NP, NP, F, EY), (2, 4, NP, F, EY), (2, 4, 2, 5, F, EY)
    small_shape = (7, ROWS, EY)
    new_wave, new_adj, sides, tops, strips, small = pl.pallas_call(
        inner_kernel,
        out_shape=(
            pltpu.HBM(field.shape, BF16),
            pltpu.HBM(field.shape, BF16),
            pltpu.HBM(side_shape, BF16),
            pltpu.HBM(top_shape, BF16),
            pltpu.HBM(strip_shape, BF16),
            pltpu.HBM(small_shape, F32),
        ),
        in_specs=[vmem] * 3 + [hbm],
        out_specs=(hbm,) * 6,
        scratch_shapes=[
            pltpu.VMEM((ROWS, EY), F32),
            pltpu.VMEM((3, ROWS, EY), F32),
            pltpu.VMEM((3, NP * ROWS, EY), BF16),
            pltpu.VMEM((2, NP, NP, NP, ROWS, EY), F32),
            pltpu.VMEM((2, NP, NP, NP, ROWS, EY), BF16),
            pltpu.VMEM((NP, NP, NP, ROWS, EY), F32),
            pltpu.VMEM((2, 4, 4, 5, F, EY), BF16),
            pltpu.VMEM(side_shape, BF16),
            pltpu.VMEM(top_shape, BF16),
            pltpu.VMEM(strip_shape, BF16),
            pltpu.VMEM(small_shape, F32),
            pltpu.VMEM(coup.shape, F32),
            pltpu.SemaphoreType.DMA((30,)),
        ],
        compiler_params=params,
        cost_estimate=pl.CostEstimate(flops=2**31, bytes_accessed=2**23, transcendentals=0),
    )(wave, adj, stiff, *far(coup))

    lam_sides, lam_tops, ends, total, own, mate = pl.pallas_call(
        trace_kernel,
        out_shape=(
            jax.ShapeDtypeStruct(side_shape[1:], BF16),
            jax.ShapeDtypeStruct((NP, NP, F, EY), BF16),
            jax.ShapeDtypeStruct((2, ROWS, EY), BF16),
            jax.ShapeDtypeStruct((F, EY), F32),
            jax.ShapeDtypeStruct((1, EY), jnp.int32),
            jax.ShapeDtypeStruct((1, EY), jnp.int32),
        ),
        in_specs=[vmem] + [hbm] * 4,
        out_specs=(vmem,) * 6,
        scratch_shapes=[
            pltpu.VMEM((NP * NP, F, EY), F32),
            pltpu.VMEM(partner.shape, jnp.int32),
            pltpu.VMEM(small_shape, F32),
            pltpu.VMEM((ROWS, EY), F32),
            pltpu.SemaphoreType.DMA((6,)),
        ],
        compiler_params=params,
        cost_estimate=pl.CostEstimate(flops=2**29, bytes_accessed=2**22, transcendentals=0),
    )(bottom, *far(adj, partner, own, small))

    send = pl.pallas_call(
        outer_kernel,
        out_shape=jax.ShapeDtypeStruct((count, 4 * ROWS, EY), BF16),
        in_specs=[vmem] * 6,
        out_specs=vmem,
        scratch_shapes=[pltpu.VMEM((ROWS, EY), F32)],
        compiler_params=params,
    )(first, second, lam_sides, ends, total, own)

    got = lax.all_to_all(send, "gy", 0, 0, tiled=True)

    new_wave, new_adj, cells = pl.pallas_call(
        last_kernel,
        out_shape=(field, field, jax.ShapeDtypeStruct((F, 1, CELLS_DEV), F32)),
        in_specs=[vmem] * 12 + [hbm] * 2,
        out_specs=(hbm,) * 3,
        scratch_shapes=[
            pltpu.VMEM((2, 2, NP, NP, F, EY), BF16),
            pltpu.VMEM((2, 2, 4, NP, F, EY), BF16),
            pltpu.VMEM((2, 4, 4, F, EY), BF16),
            pltpu.VMEM((F, 1, CELLS_DEV), F32),
            pltpu.VMEM((2, NP * NP, F, EY), F32),
            pltpu.SemaphoreType.DMA((11,)),
        ],
        input_output_aliases={12: 0, 13: 1},
        compiler_params=params,
    )(got, small, strips, sides, tops, second, first, bottom, mate, wave, lam_sides, lam_tops, new_wave, new_adj)

    new_wave = new_wave.transpose(3, 0, 1, 2, 4)[:, None, None]
    new_adj = new_adj.transpose(3, 0, 1, 2, 4)[:, None, None]
    return (new_wave, new_adj, cells.transpose(1, 0, 2)[None])


def solution(mesh):
    return jax.shard_map(
        per_device,
        mesh=mesh,
        in_specs=(
            P(None, "layer", "gx", None, None, None, "gy"),
            P(None, "layer", "gx", None, None, None, "gy"),
            P("layer", None, None, None),
            P(None, "layer", "gx", "gy"),
            P(None, "gx", "gy"),
            P("layer", "gx", "gy"),
        ),
        out_specs=(
            P(None, "layer", "gx", None, None, None, "gy"),
            P(None, "layer", "gx", None, None, None, "gy"),
            P("layer", "gx", None, "gy"),
        ),
        check_vma=False,
    )
```

```python
import functools
import math

import jax
import jax.numpy as jnp
import numpy as np
from jax import lax
from jax.experimental import pallas as pl
from jax.experimental.pallas import tpu as pltpu
from jax.sharding import PartitionSpec as P

F = 13
ROWS = 16
NP = 6
EY = 128
CELLS_DEV = 128
BOTTOM = 4
HALF = 64
S_RIGHT = 36
S_LEFT = 100
DT = 0.05
TAU = 7.5
F32 = jnp.float32
BF16 = jnp.bfloat16
VMEM_LIMIT = 40 * 1024 * 1024


def lobatto_derivative():
    outer = math.sqrt(1.0 / 3.0 + 2.0 * math.sqrt(7.0) / 21.0)
    inner = math.sqrt(1.0 / 3.0 - 2.0 * math.sqrt(7.0) / 21.0)
    nodes = np.array([-1.0, -outer, -inner, inner, outer, 1.0])
    weights = np.array(
        [
            1.0 / np.prod([nodes[col] - nodes[other] for other in range(6) if other != col])
            for col in range(6)
        ]
    )
    table = np.zeros((6, 6))
    for row_id in range(6):
        for col in range(6):
            if row_id != col:
                table[row_id, col] = weights[col] / weights[row_id] / (nodes[row_id] - nodes[col])
        table[row_id, row_id] = -np.sum(table[row_id])
    return table


def lane_ids(rows):
    return lax.broadcasted_iota(jnp.int32, (rows, EY), 1)


def load_scale(stiff_ref, scale):
    for f in range(F):
        scale[f : f + 1, :] = stiff_ref[f]
    return scale[0:F, :]


def prep_kernel(
    wave_ref, adj_ref, stiff_ref, second_ref, first_ref, bottom_ref,
    raw, low, stiff, scale, rows, trace, sems,
):
    odd = lax.rem(lax.axis_index("gx"), 2)
    near = 5 * (1 - odd)
    far = 5 * odd
    copies = []

    def send(src, dst):
        copies.append(pltpu.make_async_copy(src, dst, sems.at[len(copies)]))
        copies[-1].start()
        return copies[-1]

    arrivals = [
        send(stiff_ref, stiff),
        send(adj_ref.at[:, :, 0], low.at[1]),
        send(wave_ref.at[:, :, 0], low.at[0]),
        send(adj_ref.at[far], raw.at[1]),
        send(adj_ref.at[near], raw.at[0]),
    ]
    leaving = [send(wave_ref.at[far], second_ref.at[0]), send(wave_ref.at[near], first_ref.at[0])]
    for copy in arrivals[0:3]:
        copy.wait()
    s = load_scale(stiff, scale)
    s4 = s[0:BOTTOM]
    for part in range(2):
        for a in range(NP):
            for b in range(NP):
                x = low[part, a, b].astype(F32)[0:BOTTOM]
                if part == 1:
                    x = x * s4
                k = BOTTOM * (a * NP + b)
                rows[k : k + BOTTOM, :] = x
        trace[part] = rows[...].astype(BF16)
    for group in range(bottom_ref.shape[0]):
        leaving.append(send(trace, bottom_ref.at[group]))
    for out_ref, at in ((second_ref, 1), (first_ref, 0)):
        arrivals[4 - at].wait()
        for b in range(NP):
            for c in range(NP):
                raw[at, b, c] = (raw[at, b, c].astype(F32) * s).astype(BF16)
        leaving.append(send(raw.at[at], out_ref.at[1]))
    for copy in leaving:
        copy.wait()


def build_matrices(side, coup_ref, cs, mats):
    table = lobatto_derivative()
    cs[...] = jnp.zeros_like(cs)
    for d in range(3):
        for f in range(F):
            cs[d, f : f + 1, 0:F] = coup_ref[d, f]
    block = lane_ids(ROWS) // ROWS
    spread = []
    for i in range(NP):
        row = jnp.zeros((ROWS, EY), F32)
        for k in range(NP):
            row = jnp.where(block == k, F32(table[i, k]), row)
        spread.append(row)
    for d in range(3):
        base = cs[d]
        if side == 1:
            base = -jnp.concatenate([base, jnp.zeros((EY - ROWS, EY), F32)], axis=0).T[0:ROWS]
        wide = base
        for k in range(1, NP):
            wide = wide + pltpu.roll(base, ROWS * k, 1)
        for i in range(NP):
            mats[d, ROWS * i : ROWS * (i + 1), :] = (wide * spread[i]).astype(BF16)


def put(edge, tile, frm, to):
    return jnp.where(lane_ids(F) == to, pltpu.roll(tile, (to - frm) % EY, 1), edge)


def inner_kernel(
    wave_ref, adj_ref, stiff_ref, coup_ref, partner_hbm, owner_hbm,
    new_wave_ref, new_adj_ref, side_out_ref, top_out_ref, strip_out_ref, small_out_ref,
    scale, cs, mats, padded, packed, acc, mid, side_ref, top_ref, strip_ref, small, coup, partner_ref, owner_ref, sems,
):
    copies = []

    def send(src, dst):
        copies.append(pltpu.make_async_copy(src, dst, sems.at[len(copies)]))
        copies[-1].start()
        return copies[-1]

    arrivals = [send(coup_ref, coup), send(partner_hbm, partner_ref), send(owner_hbm, owner_ref)]
    s = load_scale(stiff_ref, scale)
    for a in range(NP):
        padded[:, a, :, :, 8:ROWS, :] = jnp.zeros((2, NP, NP, ROWS - 8, EY), F32)
        for b in range(NP):
            for c in range(NP):
                padded[0, a, b, c, 0:F, :] = wave_ref[a, b, c].astype(F32)
                padded[1, a, b, c, 0:F, :] = adj_ref[a, b, c].astype(F32) * s
        for side in range(2):
            packed[side, a] = padded[side, a].astype(BF16)
    for copy in arrivals:
        copy.wait()
    small[7, 0:1, :] = partner_ref[lax.axis_index("layer")].astype(F32)
    small[7, 1:2, :] = owner_ref[...].astype(F32)
    small[0, 0:F, :] = s

    def leave(side, a):
        out_ref = new_adj_ref if side else new_wave_ref
        if a in (0, 5):
            send(side_ref.at[side, a // 5], side_out_ref.at[side, a // 5])
        else:
            send(mid.at[side, a - 1], out_ref.at[a, 1:5, 0:5])
            send(top_ref.at[side, a - 1], top_out_ref.at[side, a - 1])
            send(strip_ref.at[side, a - 1], strip_out_ref.at[side, a - 1])

    for side in range(2):
        inner_side(
            side, adj_ref, s, coup, side_ref, top_ref, strip_ref, small,
            cs, mats, padded.at[side], packed.at[side], acc, mid, leave,
        )
    send(small, small_out_ref)
    for copy in copies[3:]:
        copy.wait()


def inner_side(
    side, adj_ref, s, coup_ref, side_ref, top_ref, strip_ref, small,
    cs, mats, padded, packed, acc, mid, leave,
):
    width = NP * ROWS
    lanes = lane_ids(F)
    row_ids = lax.broadcasted_iota(jnp.int32, (F, EY), 0)

    build_matrices(side, coup_ref, cs, mats)
    m = [mats[d][:, 0:width] for d in range(3)]
    for b in range(NP):
        right = jnp.concatenate([packed[:, b, c].reshape(width, EY) for c in range(NP)], axis=1)
        out = jnp.dot(m[0], right, preferred_element_type=F32)
        for c in range(NP):
            acc[:, b, c] = out[:, c * EY : (c + 1) * EY].reshape(NP, ROWS, EY)

    total = jnp.zeros((F, EY), F32)
    u_edge = jnp.zeros((F, EY), F32)
    lam_edge = jnp.zeros((F, EY), F32)
    edge = jnp.zeros((F, EY), F32)
    for a in range(NP):
        right = jnp.concatenate([packed[a, :, c].reshape(width, EY) for c in range(NP)], axis=1)
        along_b = jnp.dot(m[1], right, preferred_element_type=F32)
        right = jnp.concatenate([packed[a, b].reshape(width, EY) for b in range(NP)], axis=1)
        along_c = jnp.dot(m[2], right, preferred_element_type=F32)
        for b in range(NP):
            for c in range(NP):
                rate = (
                    acc[a, b, c]
                    + along_b[ROWS * b : ROWS * (b + 1), c * EY : (c + 1) * EY]
                    + along_c[ROWS * c : ROWS * (c + 1), b * EY : (b + 1) * EY]
                )[0:F]
                v = padded[a, b, c, 0:F, :]
                face = None
                own = (a in (0, 5)) + (b in (0, 5))
                if b == 0:
                    other = padded[a, 5, c, 0:F, :]
                    face = jnp.where(lanes == 0, 0.0, pltpu.roll(other, 1, 1))
                if b == 5:
                    other = padded[a, 0, c, 0:F, :]
                    face = jnp.where(lanes == EY - 1, 0.0, pltpu.roll(other, EY - 1, 1))
                if own:
                    rate = rate - (TAU * own) * v
                if face is not None:
                    rate = rate + TAU * face
                if c == 5:
                    rate = rate - jnp.where(row_ids < BOTTOM, TAU * v, 0.0)
                k = a * NP + c
                lam = adj_ref[a, b, c].astype(F32)
                if side == 0:
                    total = total + lam * rate
                    new = v + (DT * s) * rate
                else:
                    new = lam + DT * rate
                if a in (0, 5):
                    side_ref[side, a // 5, b, c] = rate.astype(BF16)
                elif c == 5:
                    top_ref[side, a - 1, b] = rate.astype(BF16)
                elif b in (0, 5):
                    strip_ref[side, a - 1, b // 5, c] = new.astype(BF16)
                else:
                    mid[side, a - 1, b - 1, c] = new.astype(BF16)
                if b == 0 and a not in (0, 5) and c != 5:
                    edge = put(edge, new, 0, HALF * (1 - side) + k)
                if b == 5 and a not in (0, 5) and c != 5:
                    edge = put(edge, new, EY - 1, HALF * side + k)
                if side == 0 and b == 0:
                    u_edge = put(u_edge, v, 0, k)
                    lam_edge = put(lam_edge, lam, 0, HALF + k)
                if side == 0 and b == 5:
                    u_edge = put(u_edge, v, EY - 1, HALF + k)
                    lam_edge = put(lam_edge, lam, EY - 1, k)
        leave(side, a)
    small[1 + side, 0:F, :] = edge
    if side == 0:
        small[3, 0:F, :] = total
        left = jnp.sum(jnp.where(lanes == 0, s, 0.0), axis=1, keepdims=True)
        right = jnp.sum(jnp.where(lanes == EY - 1, s, 0.0), axis=1, keepdims=True)
        lam_edge = jnp.where(lanes == S_RIGHT, right, jnp.where(lanes == S_LEFT, left, lam_edge))
        small[4, 0:F, :] = u_edge
        small[5, 0:F, :] = lam_edge
        small[6, 0:F, :] = jnp.where(lanes < HALF, right, left)


def load_floors(side, mate, bottom_ref, floors):
    pick = bottom_ref[0, side].astype(F32)
    for group in range(1, bottom_ref.shape[0]):
        pick = jnp.where(mate == group, bottom_ref[group, side].astype(F32), pick)
    for k in range(NP * NP):
        floors[k, 0:BOTTOM, :] = pick[BOTTOM * k : BOTTOM * (k + 1)]


def outside(side, a, b, c, odd, first_ref, second_ref, floors):
    face = None
    if a in (0, 5):
        one, two = first_ref[side, b, c], second_ref[side, b, c]
        near = jnp.where(odd, one, two) if a == 0 else jnp.where(odd, two, one)
        face = near.astype(F32)
    if c == 5:
        row_ids = lax.broadcasted_iota(jnp.int32, (F, EY), 0)
        x = jnp.where(row_ids < BOTTOM, floors[a * NP + b], 0.0)
        face = x if face is None else face + x
    return face


def trace_kernel(
    first_ref, bottom_ref, adj_ref, small_hbm,
    ends_ref, total_ref, owner_ref, mate_ref,
    floors, tile, small, sem,
):
    arrival = pltpu.make_async_copy(small_hbm, small, sem)
    arrival.start()
    floors[...] = jnp.zeros_like(floors)
    near = 5 * (1 - lax.rem(lax.axis_index("gx"), 2))
    sides = jnp.zeros((F, EY), F32)
    for b in range(NP):
        for c in range(NP):
            sides = sides + adj_ref[near, b, c].astype(F32) * first_ref[0, b, c].astype(F32)
    arrival.wait()
    mate = small[7, 0:1, :].astype(jnp.int32)
    mate_ref[...] = mate
    owner_ref[...] = small[7, 1:2, :].astype(jnp.int32)
    load_floors(0, mate, bottom_ref, floors)
    total = jnp.zeros((F, EY), F32)
    row_ids = lax.broadcasted_iota(jnp.int32, (F, EY), 0)
    for a in range(NP):
        for b in range(NP):
            total = total + adj_ref[a, b, 5].astype(F32) * floors[a * NP + b]
    total = jnp.where(row_ids < BOTTOM, total, 0.0) + sides
    total_ref[...] = small[3, 0:F, :] + TAU * total
    tile[...] = jnp.zeros_like(tile)
    for i in range(2):
        tile[0:F, :] = small[4 + i, 0:F, :]
        ends_ref[i] = tile[...].astype(BF16)


def outer_kernel(
    second_ref, adj_ref, ends_ref, total_ref, owner_ref,
    send_ref,
    tile,
):
    far = 5 * lax.rem(lax.axis_index("gx"), 2)
    total = jnp.zeros((F, EY), F32)
    for b in range(NP):
        for c in range(NP):
            total = total + adj_ref[far, b, c].astype(F32) * second_ref[0, b, c].astype(F32)
    tile[...] = jnp.zeros_like(tile)
    tile[0:F, :] = DT * (total_ref[...] + TAU * total)
    total = tile[...]
    high = total.astype(BF16)
    rest = total - high.astype(F32)
    middle = rest.astype(BF16)
    low = (rest - middle.astype(F32)).astype(BF16)
    parts = jnp.concatenate([low, middle, high], axis=0)
    owner = owner_ref[0]
    count = send_ref.shape[0]
    lane = lane_ids(1)
    own_left = jnp.sum(jnp.where(lane == 0, owner, 0), axis=1, keepdims=True).astype(F32)
    own_right = jnp.sum(jnp.where(lane == EY - 1, owner, 0), axis=1, keepdims=True).astype(F32)
    zeros = jnp.zeros((1, EY), F32)
    for i in range(2):
        for target in range(count):
            send_ref[target, (2 + i) * ROWS : (3 + i) * ROWS, :] = ends_ref[i]
    tile[F : F + 1, :] = zeros + own_left
    tile[F + 1 : F + 2, :] = zeros + own_right
    for target in range(count):
        cells = lax.broadcasted_iota(jnp.int32, (CELLS_DEV, EY), 0) + CELLS_DEV * target
        held = (cells == owner).astype(BF16)
        sums = lax.dot_general(parts, held, (((1,), (1,)), ((), ())), preferred_element_type=F32)
        sums = sums[0:ROWS] + sums[ROWS : 2 * ROWS] + sums[2 * ROWS :]
        tile[0:F, :] = sums[0:F]
        whole = tile[...]
        top = whole.astype(BF16)
        send_ref[target, 0:ROWS, :] = top
        send_ref[target, ROWS : 2 * ROWS, :] = (whole - top.astype(F32)).astype(BF16)


def last_kernel(
    got_ref, small, strip_ref, side_ref, top_ref, second_ref, first_ref, bottom_ref, mate_ref,
    wave_ref, adj_ref, old_wave_ref, old_adj_ref,
    new_wave_ref, new_adj_ref, cell_ref,
    patched, side_new, top_new, cell, floors, sems,
):
    me = lax.axis_index("gy")
    odd = lax.rem(lax.axis_index("gx"), 2) == 1
    mate = mate_ref[...]
    count = got_ref.shape[0]
    copies = []

    def send(src, dst):
        copies.append(pltpu.make_async_copy(src, dst, sems.at[len(copies)]))
        copies[-1].start()

    s = small[0, 0:F, :]
    factors = DT * s, DT

    def finished(side, a, b, c):
        rate = (side_ref[side, a // 5, b, c] if a in (0, 5) else top_ref[side, a - 1, b]).astype(F32)
        rate = rate + TAU * outside(side, a, b, c, odd, first_ref, second_ref, floors.at[side])
        return (adj_ref if side else wave_ref)[a, b, c].astype(F32) + factors[side] * rate

    for side, out_ref in ((0, new_wave_ref), (1, new_adj_ref)):
        load_floors(side, mate, bottom_ref, floors.at[side])
        for a in range(NP):
            for b in range(1, 5):
                if a in (0, 5):
                    for c in range(NP):
                        side_new[side, a // 5, b - 1, c] = finished(side, a, b, c).astype(BF16)
                else:
                    top_new[side, a - 1, b - 1] = finished(side, a, b, 5).astype(BF16)
            if a in (0, 5):
                send(side_new.at[side, a // 5], out_ref.at[a, 1:5])
        send(top_new.at[side], out_ref.at[1:5, 1:5, 5])
    lanes = lane_ids(F)
    upper = lanes >= HALF

    def tile(j, i):
        return got_ref[j, ROWS * i : ROWS * (i + 1), :].astype(F32)

    cells = jnp.zeros((F, EY), F32)
    lane = (lane_ids(1) + CELLS_DEV * me).astype(F32)
    for j in range(count):
        sums = tile(j, 0) + tile(j, 1)
        cells = cells + sums[0:F]
        lam = tile(j, 3)[0:F]
        for other, side, row in ((j - 1, upper, F), (j + 1, lanes < HALF, F + 1)):
            if 0 <= other < count:
                pairs = jnp.where(side, lam * tile(other, 2)[0:F], 0.0)
                value = (DT * TAU) * jnp.sum(pairs, axis=1, keepdims=True)
                cells = cells + jnp.where(sums[row : row + 1] == lane, value, 0.0)
    for f in range(F):
        cell[f] = cells[f : f + 1]
    send(cell, cell_ref)

    below = lax.max(me - 1, 0)
    above = lax.min(me + 1, count - 1)

    def held(values, column):
        return jnp.sum(jnp.where(lanes == column, values, 0.0), axis=1, keepdims=True)

    for side, out_ref in ((0, new_wave_ref), (1, new_adj_ref)):
        low = jnp.where(me > 0, tile(below, 2 + side)[0:F], 0.0)
        high = jnp.where(me < count - 1, tile(above, 2 + side)[0:F], 0.0)
        if side == 0:
            near = jnp.where(upper, low, high) * small[6, 0:F, :]
        else:
            near = jnp.where(upper, high * held(high, S_LEFT), low * held(low, S_RIGHT))
        near = (DT * TAU) * near
        edge = small[1 + side, 0:F, :] + near
        for b, end, start in ((0, 0, HALF if side == 0 else 0), (1, EY - 1, 0 if side == 0 else HALF)):
            for a in range(NP):
                for c in range(NP):
                    shift = (end - start - a * NP - c) % EY
                    if a in (0, 5) or c == 5:
                        old = finished(side, a, 5 * b, c)
                        moved = old + pltpu.roll(near, shift, 1)
                    else:
                        old = strip_ref[side, a - 1, b, c].astype(F32)
                        moved = pltpu.roll(edge, shift, 1)
                    patched[side, b, a, c] = jnp.where(lanes == end, moved, old).astype(BF16)
            send(patched.at[side, b], out_ref.at[:, 5 * b])
    for copy in copies:
        copy.wait()


def swap(x, axis, pairs):
    return lax.ppermute(x, axis, [(i, j) for i, j in pairs] + [(j, i) for i, j in pairs])


def per_device(wave, adjoint_source, coupling, stiffness, partner, owner):
    wave = wave[:, 0, 0].transpose(1, 2, 3, 0, 4)
    adj = adjoint_source[:, 0, 0].transpose(1, 2, 3, 0, 4)
    stiff = stiffness[:, 0]
    coup = coupling[0][:, :, None, :]
    own = owner[0]
    layers, columns, count = (lax.axis_size(axis) for axis in ("layer", "gx", "gy"))
    field = jax.ShapeDtypeStruct((NP, NP, NP, F, EY), BF16)
    faces = jax.ShapeDtypeStruct((2, NP, NP, F, EY), BF16)
    traces = jax.ShapeDtypeStruct((layers, 2, BOTTOM * NP * NP, EY), BF16)
    vmem = pl.BlockSpec(memory_space=pltpu.VMEM)
    hbm = pl.BlockSpec(memory_space=pltpu.HBM)
    params = pltpu.CompilerParams(vmem_limit_bytes=VMEM_LIMIT)

    def far(*arrays):
        return tuple(pltpu.with_memory_space_constraint(x, pltpu.HBM) for x in arrays)

    second, first, bottom = pl.pallas_call(
        prep_kernel,
        out_shape=(faces, faces, traces),
        in_specs=[hbm] * 3,
        out_specs=(hbm,) * 3,
        scratch_shapes=[
            pltpu.VMEM((2, NP, NP, F, EY), BF16),
            pltpu.VMEM((2, NP, NP, F, EY), BF16),
            pltpu.VMEM((F, 1, EY), F32),
            pltpu.VMEM((ROWS, EY), F32),
            pltpu.VMEM((BOTTOM * NP * NP, EY), F32),
            pltpu.VMEM(traces.shape[1:], BF16),
            pltpu.SemaphoreType.DMA((9 + layers,)),
        ],
        compiler_params=params,
    )(*far(wave, adj, stiff))

    second = swap(second, "gx", [(i, i + 1) for i in range(1, columns - 1, 2)])
    first = swap(first, "gx", [(i, i + 1) for i in range(0, columns - 1, 2)])
    bottom = lax.all_to_all(bottom, "layer", 0, 0, tiled=True)

    side_shape, top_shape, strip_shape = (2, 2, NP, NP, F, EY), (2, 4, NP, F, EY), (2, 4, 2, 5, F, EY)
    small_shape = (8, ROWS, EY)
    new_wave, new_adj, sides, tops, strips, small = pl.pallas_call(
        inner_kernel,
        out_shape=(
            pltpu.HBM(field.shape, BF16),
            pltpu.HBM(field.shape, BF16),
            pltpu.HBM(side_shape, BF16),
            pltpu.HBM(top_shape, BF16),
            pltpu.HBM(strip_shape, BF16),
            pltpu.HBM(small_shape, F32),
        ),
        in_specs=[vmem] * 3 + [hbm] * 3,
        out_specs=(hbm,) * 6,
        scratch_shapes=[
            pltpu.VMEM((ROWS, EY), F32),
            pltpu.VMEM((3, ROWS, EY), F32),
            pltpu.VMEM((3, NP * ROWS, EY), BF16),
            pltpu.VMEM((2, NP, NP, NP, ROWS, EY), F32),
            pltpu.VMEM((2, NP, NP, NP, ROWS, EY), BF16),
            pltpu.VMEM((NP, NP, NP, ROWS, EY), F32),
            pltpu.VMEM((2, 4, 4, 5, F, EY), BF16),
            pltpu.VMEM(side_shape, BF16),
            pltpu.VMEM(top_shape, BF16),
            pltpu.VMEM(strip_shape, BF16),
            pltpu.VMEM(small_shape, F32),
            pltpu.VMEM(coup.shape, F32),
            pltpu.VMEM(partner.shape, jnp.int32),
            pltpu.VMEM(own.shape, jnp.int32),
            pltpu.SemaphoreType.DMA((32,)),
        ],
        compiler_params=params,
        cost_estimate=pl.CostEstimate(flops=2**31, bytes_accessed=2**23, transcendentals=0),
    )(wave, adj, stiff, *far(coup, partner, own))

    ends, total, own, mate = pl.pallas_call(
        trace_kernel,
        out_shape=(
            jax.ShapeDtypeStruct((2, ROWS, EY), BF16),
            jax.ShapeDtypeStruct((F, EY), F32),
            jax.ShapeDtypeStruct((1, EY), jnp.int32),
            jax.ShapeDtypeStruct((1, EY), jnp.int32),
        ),
        in_specs=[vmem] * 3 + [hbm],
        out_specs=(vmem,) * 4,
        scratch_shapes=[
            pltpu.VMEM((NP * NP, F, EY), F32),
            pltpu.VMEM((ROWS, EY), F32),
            pltpu.VMEM(small_shape, F32),
            pltpu.SemaphoreType.DMA,
        ],
        compiler_params=params,
        cost_estimate=pl.CostEstimate(flops=2**29, bytes_accessed=2**22, transcendentals=0),
    )(first, bottom, adj, *far(small))

    send = pl.pallas_call(
        outer_kernel,
        out_shape=jax.ShapeDtypeStruct((count, 4 * ROWS, EY), BF16),
        in_specs=[vmem] * 5,
        out_specs=vmem,
        scratch_shapes=[pltpu.VMEM((ROWS, EY), F32)],
        compiler_params=params,
    )(second, adj, ends, total, own)

    got = lax.all_to_all(send, "gy", 0, 0, tiled=True)

    new_wave, new_adj, cells = pl.pallas_call(
        last_kernel,
        out_shape=(field, field, jax.ShapeDtypeStruct((F, 1, CELLS_DEV), F32)),
        in_specs=[vmem] * 11 + [hbm] * 2,
        out_specs=(hbm,) * 3,
        scratch_shapes=[
            pltpu.VMEM((2, 2, NP, NP, F, EY), BF16),
            pltpu.VMEM((2, 2, 4, NP, F, EY), BF16),
            pltpu.VMEM((2, 4, 4, F, EY), BF16),
            pltpu.VMEM((F, 1, CELLS_DEV), F32),
            pltpu.VMEM((2, NP * NP, F, EY), F32),
            pltpu.SemaphoreType.DMA((11,)),
        ],
        input_output_aliases={11: 0, 12: 1},
        compiler_params=params,
    )(got, small, strips, sides, tops, second, first, bottom, mate, wave, adj, new_wave, new_adj)

    new_wave = new_wave.transpose(3, 0, 1, 2, 4)[:, None, None]
    new_adj = new_adj.transpose(3, 0, 1, 2, 4)[:, None, None]
    return (new_wave, new_adj, cells.transpose(1, 0, 2)[None])


def solution(mesh):
    return jax.shard_map(
        per_device,
        mesh=mesh,
        in_specs=(
            P(None, "layer", "gx", None, None, None, "gy"),
            P(None, "layer", "gx", None, None, None, "gy"),
            P("layer", None, None, None),
            P(None, "layer", "gx", "gy"),
            P(None, "gx", "gy"),
            P("layer", "gx", "gy"),
        ),
        out_specs=(
            P(None, "layer", "gx", None, None, None, "gy"),
            P(None, "layer", "gx", None, None, None, "gy"),
            P("layer", "gx", None, "gy"),
        ),
        check_vma=False,
    )
```

```python
import functools
import math

import jax
import jax.numpy as jnp
import numpy as np
from jax import lax
from jax.experimental import pallas as pl
from jax.experimental.pallas import tpu as pltpu
from jax.sharding import PartitionSpec as P

F = 13
ROWS = 16
NP = 6
EY = 128
CELLS_DEV = 128
BOTTOM = 4
HALF = 64
S_RIGHT = 36
S_LEFT = 100
DT = 0.05
TAU = 7.5
F32 = jnp.float32
BF16 = jnp.bfloat16
VMEM_LIMIT = 40 * 1024 * 1024


def lobatto_derivative():
    outer = math.sqrt(1.0 / 3.0 + 2.0 * math.sqrt(7.0) / 21.0)
    inner = math.sqrt(1.0 / 3.0 - 2.0 * math.sqrt(7.0) / 21.0)
    nodes = np.array([-1.0, -outer, -inner, inner, outer, 1.0])
    weights = np.array(
        [
            1.0 / np.prod([nodes[col] - nodes[other] for other in range(6) if other != col])
            for col in range(6)
        ]
    )
    table = np.zeros((6, 6))
    for row_id in range(6):
        for col in range(6):
            if row_id != col:
                table[row_id, col] = weights[col] / weights[row_id] / (nodes[row_id] - nodes[col])
        table[row_id, row_id] = -np.sum(table[row_id])
    return table


def lane_ids(rows):
    return lax.broadcasted_iota(jnp.int32, (rows, EY), 1)


def load_scale(stiff_ref, scale):
    for f in range(F):
        scale[f : f + 1, :] = stiff_ref[f]
    return scale[0:F, :]


def prep_kernel(
    wave_ref, adj_ref, stiff_ref, second_ref, first_ref, bottom_ref,
    raw, low, stiff, scale, rows, trace, sems,
):
    odd = lax.rem(lax.axis_index("gx"), 2)
    near = 5 * (1 - odd)
    far = 5 * odd
    copies = []

    def send(src, dst):
        copies.append(pltpu.make_async_copy(src, dst, sems.at[len(copies)]))
        copies[-1].start()
        return copies[-1]

    arrivals = [
        send(stiff_ref, stiff),
        send(adj_ref.at[:, :, 0], low.at[1]),
        send(wave_ref.at[:, :, 0], low.at[0]),
        send(adj_ref.at[far], raw.at[1]),
        send(adj_ref.at[near], raw.at[0]),
    ]
    leaving = [send(wave_ref.at[far], second_ref.at[0]), send(wave_ref.at[near], first_ref.at[0])]
    for copy in arrivals[0:3]:
        copy.wait()
    s = load_scale(stiff, scale)
    s4 = s[0:BOTTOM]
    for part in range(2):
        for a in range(NP):
            for b in range(NP):
                x = low[part, a, b].astype(F32)[0:BOTTOM]
                if part == 1:
                    x = x * s4
                k = BOTTOM * (a * NP + b)
                rows[k : k + BOTTOM, :] = x
        trace[part] = rows[...].astype(BF16)
    for group in range(bottom_ref.shape[0]):
        leaving.append(send(trace, bottom_ref.at[group]))
    for out_ref, at in ((second_ref, 1), (first_ref, 0)):
        arrivals[4 - at].wait()
        for b in range(NP):
            for c in range(NP):
                raw[at, b, c] = (raw[at, b, c].astype(F32) * s).astype(BF16)
        leaving.append(send(raw.at[at], out_ref.at[1]))
    for copy in leaving:
        copy.wait()


def build_matrices(side, coup_ref, cs, mats):
    table = lobatto_derivative()
    cs[...] = jnp.zeros_like(cs)
    for d in range(3):
        for f in range(F):
            cs[d, f : f + 1, 0:F] = coup_ref[d, f]
    block = lane_ids(ROWS) // ROWS
    spread = []
    for i in range(NP):
        row = jnp.zeros((ROWS, EY), F32)
        for k in range(NP):
            row = jnp.where(block == k, F32(table[i, k]), row)
        spread.append(row)
    for d in range(3):
        base = cs[d]
        if side == 1:
            base = -jnp.concatenate([base, jnp.zeros((EY - ROWS, EY), F32)], axis=0).T[0:ROWS]
        wide = base
        for k in range(1, NP):
            wide = wide + pltpu.roll(base, ROWS * k, 1)
        for i in range(NP):
            mats[d, ROWS * i : ROWS * (i + 1), :] = (wide * spread[i]).astype(BF16)


def put(edge, tile, frm, to):
    return jnp.where(lane_ids(F) == to, pltpu.roll(tile, (to - frm) % EY, 1), edge)


def inner_kernel(
    wave_ref, adj_ref, stiff_ref, coup_ref, partner_hbm, owner_hbm,
    new_wave_ref, new_adj_ref, side_out_ref, top_out_ref, strip_out_ref, small_out_ref,
    scale, cs, mats, padded, packed, acc, mid, side_ref, top_ref, strip_ref, small, coup, partner_ref, owner_ref, sems,
):
    copies = []

    def send(src, dst):
        copies.append(pltpu.make_async_copy(src, dst, sems.at[len(copies)]))
        copies[-1].start()
        return copies[-1]

    arrivals = [send(coup_ref, coup), send(partner_hbm, partner_ref), send(owner_hbm, owner_ref)]
    s = load_scale(stiff_ref, scale)
    for a in range(NP):
        padded[:, a, :, :, 8:ROWS, :] = jnp.zeros((2, NP, NP, ROWS - 8, EY), F32)
        for b in range(NP):
            for c in range(NP):
                padded[0, a, b, c, 0:F, :] = wave_ref[a, b, c].astype(F32)
                padded[1, a, b, c, 0:F, :] = adj_ref[a, b, c].astype(F32) * s
        for side in range(2):
            packed[side, a] = padded[side, a].astype(BF16)
    for copy in arrivals:
        copy.wait()
    small[7, 0:1, :] = partner_ref[lax.axis_index("layer")].astype(F32)
    small[7, 1:2, :] = owner_ref[...].astype(F32)
    small[0, 0:F, :] = s

    def leave(side, a):
        out_ref = new_adj_ref if side else new_wave_ref
        if a in (0, 5):
            send(side_ref.at[side, a // 5], side_out_ref.at[side, a // 5])
        else:
            send(mid.at[side, a - 1], out_ref.at[a, 1:5, 0:5])
            send(top_ref.at[side, a - 1], top_out_ref.at[side, a - 1])
            send(strip_ref.at[side, a - 1], strip_out_ref.at[side, a - 1])

    for side in range(2):
        inner_side(
            side, adj_ref, s, coup, side_ref, top_ref, strip_ref, small,
            cs, mats, padded.at[side], packed.at[side], acc, mid, leave,
        )
    send(small, small_out_ref)
    for copy in copies[3:]:
        copy.wait()


def inner_side(
    side, adj_ref, s, coup_ref, side_ref, top_ref, strip_ref, small,
    cs, mats, padded, packed, acc, mid, leave,
):
    width = NP * ROWS
    lanes = lane_ids(F)
    row_ids = lax.broadcasted_iota(jnp.int32, (F, EY), 0)

    build_matrices(side, coup_ref, cs, mats)
    m = [mats[d][:, 0:width] for d in range(3)]
    for b in range(NP):
        right = jnp.concatenate([packed[:, b, c].reshape(width, EY) for c in range(NP)], axis=1)
        out = jnp.dot(m[0], right, preferred_element_type=F32)
        for c in range(NP):
            acc[:, b, c] = out[:, c * EY : (c + 1) * EY].reshape(NP, ROWS, EY)

    total = jnp.zeros((F, EY), F32)
    u_edge = jnp.zeros((F, EY), F32)
    lam_edge = jnp.zeros((F, EY), F32)
    edge = jnp.zeros((F, EY), F32)
    for a in range(NP):
        right = jnp.concatenate([packed[a, :, c].reshape(width, EY) for c in range(NP)], axis=1)
        along_b = jnp.dot(m[1], right, preferred_element_type=F32)
        right = jnp.concatenate([packed[a, b].reshape(width, EY) for b in range(NP)], axis=1)
        along_c = jnp.dot(m[2], right, preferred_element_type=F32)
        for b in range(NP):
            for c in range(NP):
                rate = (
                    acc[a, b, c]
                    + along_b[ROWS * b : ROWS * (b + 1), c * EY : (c + 1) * EY]
                    + along_c[ROWS * c : ROWS * (c + 1), b * EY : (b + 1) * EY]
                )[0:F]
                v = padded[a, b, c, 0:F, :]
                face = None
                own = (a in (0, 5)) + (b in (0, 5))
                if b == 0:
                    other = padded[a, 5, c, 0:F, :]
                    face = jnp.where(lanes == 0, 0.0, pltpu.roll(other, 1, 1))
                if b == 5:
                    other = padded[a, 0, c, 0:F, :]
                    face = jnp.where(lanes == EY - 1, 0.0, pltpu.roll(other, EY - 1, 1))
                if own:
                    rate = rate - (TAU * own) * v
                if face is not None:
                    rate = rate + TAU * face
                if c == 5:
                    rate = rate - jnp.where(row_ids < BOTTOM, TAU * v, 0.0)
                k = a * NP + c
                lam = adj_ref[a, b, c].astype(F32)
                if side == 0:
                    total = total + lam * rate
                    new = v + (DT * s) * rate
                else:
                    new = lam + DT * rate
                if a in (0, 5):
                    side_ref[side, a // 5, b, c] = rate.astype(BF16)
                elif c == 5:
                    top_ref[side, a - 1, b] = rate.astype(BF16)
                elif b in (0, 5):
                    strip_ref[side, a - 1, b // 5, c] = new.astype(BF16)
                else:
                    mid[side, a - 1, b - 1, c] = new.astype(BF16)
                if b == 0 and a not in (0, 5) and c != 5:
                    edge = put(edge, new, 0, HALF * (1 - side) + k)
                if b == 5 and a not in (0, 5) and c != 5:
                    edge = put(edge, new, EY - 1, HALF * side + k)
                if side == 0 and b == 0:
                    u_edge = put(u_edge, v, 0, k)
                    lam_edge = put(lam_edge, lam, 0, HALF + k)
                if side == 0 and b == 5:
                    u_edge = put(u_edge, v, EY - 1, HALF + k)
                    lam_edge = put(lam_edge, lam, EY - 1, k)
        leave(side, a)
    small[1 + side, 0:F, :] = edge
    if side == 0:
        small[3, 0:F, :] = total
        left = jnp.sum(jnp.where(lanes == 0, s, 0.0), axis=1, keepdims=True)
        right = jnp.sum(jnp.where(lanes == EY - 1, s, 0.0), axis=1, keepdims=True)
        lam_edge = jnp.where(lanes == S_RIGHT, right, jnp.where(lanes == S_LEFT, left, lam_edge))
        small[4, 0:F, :] = u_edge
        small[5, 0:F, :] = lam_edge
        small[6, 0:F, :] = jnp.where(lanes < HALF, right, left)


def load_floors(side, mate, bottom_ref, floors):
    pick = bottom_ref[0, side].astype(F32)
    for group in range(1, bottom_ref.shape[0]):
        pick = jnp.where(mate == group, bottom_ref[group, side].astype(F32), pick)
    for k in range(NP * NP):
        floors[k, 0:BOTTOM, :] = pick[BOTTOM * k : BOTTOM * (k + 1)]


def outside(side, a, b, c, odd, first_ref, second_ref, floors):
    face = None
    if a in (0, 5):
        one, two = first_ref[side, b, c], second_ref[side, b, c]
        near = jnp.where(odd, one, two) if a == 0 else jnp.where(odd, two, one)
        face = near.astype(F32)
    if c == 5:
        row_ids = lax.broadcasted_iota(jnp.int32, (F, EY), 0)
        x = jnp.where(row_ids < BOTTOM, floors[a * NP + b], 0.0)
        face = x if face is None else face + x
    return face


def trace_kernel(
    first_ref, bottom_ref, adj_ref, small_hbm,
    ends_ref, total_ref, owner_ref, mate_ref,
    floors, tile, small, sem,
):
    arrival = pltpu.make_async_copy(small_hbm, small, sem)
    arrival.start()
    floors[...] = jnp.zeros_like(floors)
    near = 5 * (1 - lax.rem(lax.axis_index("gx"), 2))
    sides = jnp.zeros((F, EY), F32)
    for b in range(NP):
        for c in range(NP):
            sides = sides + adj_ref[near, b, c].astype(F32) * first_ref[0, b, c].astype(F32)
    arrival.wait()
    mate = small[7, 0:1, :].astype(jnp.int32)
    mate_ref[...] = mate
    owner_ref[...] = small[7, 1:2, :].astype(jnp.int32)
    load_floors(0, mate, bottom_ref, floors)
    total = jnp.zeros((F, EY), F32)
    row_ids = lax.broadcasted_iota(jnp.int32, (F, EY), 0)
    for a in range(NP):
        for b in range(NP):
            total = total + adj_ref[a, b, 5].astype(F32) * floors[a * NP + b]
    total = jnp.where(row_ids < BOTTOM, total, 0.0) + sides
    total_ref[...] = small[3, 0:F, :] + TAU * total
    tile[...] = jnp.zeros_like(tile)
    for i in range(2):
        tile[0:F, :] = small[4 + i, 0:F, :]
        ends_ref[i] = tile[...].astype(BF16)


def outer_kernel(
    second_ref, adj_ref, ends_ref, total_ref, owner_ref,
    send_ref,
    tile,
):
    far = 5 * lax.rem(lax.axis_index("gx"), 2)
    total = jnp.zeros((F, EY), F32)
    for b in range(NP):
        for c in range(NP):
            total = total + adj_ref[far, b, c].astype(F32) * second_ref[0, b, c].astype(F32)
    tile[...] = jnp.zeros_like(tile)
    tile[0:F, :] = DT * (total_ref[...] + TAU * total)
    total = tile[...]
    high = total.astype(BF16)
    rest = total - high.astype(F32)
    middle = rest.astype(BF16)
    low = (rest - middle.astype(F32)).astype(BF16)
    parts = jnp.concatenate([low, middle, high], axis=0)
    owner = owner_ref[0]
    count = send_ref.shape[0]
    lane = lane_ids(1)
    own_left = jnp.sum(jnp.where(lane == 0, owner, 0), axis=1, keepdims=True)
    own_right = jnp.sum(jnp.where(lane == EY - 1, owner, 0), axis=1, keepdims=True)
    for i in range(2):
        for target in range(count):
            send_ref[target, (1 + i) * ROWS : (2 + i) * ROWS, :] = ends_ref[i]
    for i, own in enumerate((own_left, own_right)):
        tile[F + i : F + i + 1, :] = jnp.where(lane < HALF, own >> 7, own & 127).astype(F32)
    for target in range(count):
        cells = lax.broadcasted_iota(jnp.int32, (CELLS_DEV, EY), 0) + CELLS_DEV * target
        held = (cells == owner).astype(BF16)
        sums = lax.dot_general(parts, held, (((1,), (1,)), ((), ())), preferred_element_type=F32)
        sums = sums[0:ROWS] + sums[ROWS : 2 * ROWS] + sums[2 * ROWS :]
        tile[0:F, :] = sums[0:F]
        send_ref[target, 0:ROWS, :] = tile[...].astype(BF16)


def last_kernel(
    got_ref, small, strip_ref, side_ref, top_ref, second_ref, first_ref, bottom_ref, mate_ref,
    wave_ref, adj_ref, old_wave_ref, old_adj_ref,
    new_wave_ref, new_adj_ref, cell_ref,
    patched, side_new, top_new, cell, floors, sems,
):
    me = lax.axis_index("gy")
    odd = lax.rem(lax.axis_index("gx"), 2) == 1
    mate = mate_ref[...]
    count = got_ref.shape[0]
    copies = []

    def send(src, dst):
        copies.append(pltpu.make_async_copy(src, dst, sems.at[len(copies)]))
        copies[-1].start()

    s = small[0, 0:F, :]
    factors = DT * s, DT

    def finished(side, a, b, c):
        rate = (side_ref[side, a // 5, b, c] if a in (0, 5) else top_ref[side, a - 1, b]).astype(F32)
        rate = rate + TAU * outside(side, a, b, c, odd, first_ref, second_ref, floors.at[side])
        return (adj_ref if side else wave_ref)[a, b, c].astype(F32) + factors[side] * rate

    for side, out_ref in ((0, new_wave_ref), (1, new_adj_ref)):
        load_floors(side, mate, bottom_ref, floors.at[side])
        for a in range(NP):
            for b in range(1, 5):
                if a in (0, 5):
                    for c in range(NP):
                        side_new[side, a // 5, b - 1, c] = finished(side, a, b, c).astype(BF16)
                else:
                    top_new[side, a - 1, b - 1] = finished(side, a, b, 5).astype(BF16)
            if a in (0, 5):
                send(side_new.at[side, a // 5], out_ref.at[a, 1:5])
        send(top_new.at[side], out_ref.at[1:5, 1:5, 5])
    lanes = lane_ids(F)
    upper = lanes >= HALF

    def tile(j, i):
        return got_ref[j, ROWS * i : ROWS * (i + 1), :].astype(F32)

    cells = jnp.zeros((F, EY), F32)
    lane = lane_ids(1).astype(F32)
    for j in range(count):
        sums = tile(j, 0)
        cells = cells + sums[0:F]
        lam = tile(j, 2)[0:F]
        for other, side, row in ((j - 1, upper, F), (j + 1, lanes < HALF, F + 1)):
            if 0 <= other < count:
                pairs = jnp.where(side, lam * tile(other, 1)[0:F], 0.0)
                value = (DT * TAU) * jnp.sum(pairs, axis=1, keepdims=True)
                place = sums[row : row + 1]
                hit = (place[:, 0:1] == me.astype(F32)) & (place[:, HALF : HALF + 1] == lane)
                cells = cells + jnp.where(hit, value, 0.0)
    for f in range(F):
        cell[f] = cells[f : f + 1]
    send(cell, cell_ref)

    below = lax.max(me - 1, 0)
    above = lax.min(me + 1, count - 1)

    def held(values, column):
        return jnp.sum(jnp.where(lanes == column, values, 0.0), axis=1, keepdims=True)

    for side, out_ref in ((0, new_wave_ref), (1, new_adj_ref)):
        low = jnp.where(me > 0, tile(below, 1 + side)[0:F], 0.0)
        high = jnp.where(me < count - 1, tile(above, 1 + side)[0:F], 0.0)
        if side == 0:
            near = jnp.where(upper, low, high) * small[6, 0:F, :]
        else:
            near = jnp.where(upper, high * held(high, S_LEFT), low * held(low, S_RIGHT))
        near = (DT * TAU) * near
        edge = small[1 + side, 0:F, :] + near
        for b, end, start in ((0, 0, HALF if side == 0 else 0), (1, EY - 1, 0 if side == 0 else HALF)):
            for a in range(NP):
                for c in range(NP):
                    shift = (end - start - a * NP - c) % EY
                    if a in (0, 5) or c == 5:
                        old = finished(side, a, 5 * b, c)
                        moved = old + pltpu.roll(near, shift, 1)
                    else:
                        old = strip_ref[side, a - 1, b, c].astype(F32)
                        moved = pltpu.roll(edge, shift, 1)
                    patched[side, b, a, c] = jnp.where(lanes == end, moved, old).astype(BF16)
            send(patched.at[side, b], out_ref.at[:, 5 * b])
    for copy in copies:
        copy.wait()


def swap(x, axis, pairs):
    return lax.ppermute(x, axis, [(i, j) for i, j in pairs] + [(j, i) for i, j in pairs])


def per_device(wave, adjoint_source, coupling, stiffness, partner, owner):
    wave = wave[:, 0, 0].transpose(1, 2, 3, 0, 4)
    adj = adjoint_source[:, 0, 0].transpose(1, 2, 3, 0, 4)
    stiff = stiffness[:, 0]
    coup = coupling[0][:, :, None, :]
    own = owner[0]
    layers, columns, count = (lax.axis_size(axis) for axis in ("layer", "gx", "gy"))
    field = jax.ShapeDtypeStruct((NP, NP, NP, F, EY), BF16)
    faces = jax.ShapeDtypeStruct((2, NP, NP, F, EY), BF16)
    traces = jax.ShapeDtypeStruct((layers, 2, BOTTOM * NP * NP, EY), BF16)
    vmem = pl.BlockSpec(memory_space=pltpu.VMEM)
    hbm = pl.BlockSpec(memory_space=pltpu.HBM)
    params = pltpu.CompilerParams(vmem_limit_bytes=VMEM_LIMIT)

    def far(*arrays):
        return tuple(pltpu.with_memory_space_constraint(x, pltpu.HBM) for x in arrays)

    second, first, bottom = pl.pallas_call(
        prep_kernel,
        out_shape=(faces, faces, traces),
        in_specs=[hbm] * 3,
        out_specs=(hbm,) * 3,
        scratch_shapes=[
            pltpu.VMEM((2, NP, NP, F, EY), BF16),
            pltpu.VMEM((2, NP, NP, F, EY), BF16),
            pltpu.VMEM((F, 1, EY), F32),
            pltpu.VMEM((ROWS, EY), F32),
            pltpu.VMEM((BOTTOM * NP * NP, EY), F32),
            pltpu.VMEM(traces.shape[1:], BF16),
            pltpu.SemaphoreType.DMA((9 + layers,)),
        ],
        compiler_params=params,
    )(*far(wave, adj, stiff))

    second = swap(second, "gx", [(i, i + 1) for i in range(1, columns - 1, 2)])
    first = swap(first, "gx", [(i, i + 1) for i in range(0, columns - 1, 2)])
    bottom = lax.all_to_all(bottom, "layer", 0, 0, tiled=True)

    side_shape, top_shape, strip_shape = (2, 2, NP, NP, F, EY), (2, 4, NP, F, EY), (2, 4, 2, 5, F, EY)
    small_shape = (8, ROWS, EY)
    new_wave, new_adj, sides, tops, strips, small = pl.pallas_call(
        inner_kernel,
        out_shape=(
            pltpu.HBM(field.shape, BF16),
            pltpu.HBM(field.shape, BF16),
            pltpu.HBM(side_shape, BF16),
            pltpu.HBM(top_shape, BF16),
            pltpu.HBM(strip_shape, BF16),
            pltpu.HBM(small_shape, F32),
        ),
        in_specs=[vmem] * 3 + [hbm] * 3,
        out_specs=(hbm,) * 6,
        scratch_shapes=[
            pltpu.VMEM((ROWS, EY), F32),
            pltpu.VMEM((3, ROWS, EY), F32),
            pltpu.VMEM((3, NP * ROWS, EY), BF16),
            pltpu.VMEM((2, NP, NP, NP, ROWS, EY), F32),
            pltpu.VMEM((2, NP, NP, NP, ROWS, EY), BF16),
            pltpu.VMEM((NP, NP, NP, ROWS, EY), F32),
            pltpu.VMEM((2, 4, 4, 5, F, EY), BF16),
            pltpu.VMEM(side_shape, BF16),
            pltpu.VMEM(top_shape, BF16),
            pltpu.VMEM(strip_shape, BF16),
            pltpu.VMEM(small_shape, F32),
            pltpu.VMEM(coup.shape, F32),
            pltpu.VMEM(partner.shape, jnp.int32),
            pltpu.VMEM(own.shape, jnp.int32),
            pltpu.SemaphoreType.DMA((32,)),
        ],
        compiler_params=params,
        cost_estimate=pl.CostEstimate(flops=2**31, bytes_accessed=2**23, transcendentals=0),
    )(wave, adj, stiff, *far(coup, partner, own))

    ends, total, own, mate = pl.pallas_call(
        trace_kernel,
        out_shape=(
            jax.ShapeDtypeStruct((2, ROWS, EY), BF16),
            jax.ShapeDtypeStruct((F, EY), F32),
            jax.ShapeDtypeStruct((1, EY), jnp.int32),
            jax.ShapeDtypeStruct((1, EY), jnp.int32),
        ),
        in_specs=[vmem] * 3 + [hbm],
        out_specs=(vmem,) * 4,
        scratch_shapes=[
            pltpu.VMEM((NP * NP, F, EY), F32),
            pltpu.VMEM((ROWS, EY), F32),
            pltpu.VMEM(small_shape, F32),
            pltpu.SemaphoreType.DMA,
        ],
        compiler_params=params,
        cost_estimate=pl.CostEstimate(flops=2**29, bytes_accessed=2**22, transcendentals=0),
    )(first, bottom, adj, *far(small))

    send = pl.pallas_call(
        outer_kernel,
        out_shape=jax.ShapeDtypeStruct((count, 3 * ROWS, EY), BF16),
        in_specs=[vmem] * 5,
        out_specs=vmem,
        scratch_shapes=[pltpu.VMEM((ROWS, EY), F32)],
        compiler_params=params,
    )(second, adj, ends, total, own)

    got = lax.all_to_all(send, "gy", 0, 0, tiled=True)

    new_wave, new_adj, cells = pl.pallas_call(
        last_kernel,
        out_shape=(field, field, jax.ShapeDtypeStruct((F, 1, CELLS_DEV), F32)),
        in_specs=[vmem] * 11 + [hbm] * 2,
        out_specs=(hbm,) * 3,
        scratch_shapes=[
            pltpu.VMEM((2, 2, NP, NP, F, EY), BF16),
            pltpu.VMEM((2, 2, 4, NP, F, EY), BF16),
            pltpu.VMEM((2, 4, 4, F, EY), BF16),
            pltpu.VMEM((F, 1, CELLS_DEV), F32),
            pltpu.VMEM((2, NP * NP, F, EY), F32),
            pltpu.SemaphoreType.DMA((11,)),
        ],
        input_output_aliases={11: 0, 12: 1},
        compiler_params=params,
    )(got, small, strips, sides, tops, second, first, bottom, mate, wave, adj, new_wave, new_adj)

    new_wave = new_wave.transpose(3, 0, 1, 2, 4)[:, None, None]
    new_adj = new_adj.transpose(3, 0, 1, 2, 4)[:, None, None]
    return (new_wave, new_adj, cells.transpose(1, 0, 2)[None])


def solution(mesh):
    return jax.shard_map(
        per_device,
        mesh=mesh,
        in_specs=(
            P(None, "layer", "gx", None, None, None, "gy"),
            P(None, "layer", "gx", None, None, None, "gy"),
            P("layer", None, None, None),
            P(None, "layer", "gx", "gy"),
            P(None, "gx", "gy"),
            P("layer", "gx", "gy"),
        ),
        out_specs=(
            P(None, "layer", "gx", None, None, None, "gy"),
            P(None, "layer", "gx", None, None, None, "gy"),
            P("layer", "gx", None, "gy"),
        ),
        check_vma=False,
    )
```
